256 devices in a mesh: row: 16 (over x_hi, z), col: 16 (over x_lo, y, core).
Axes of the slice: x: 4 (x_hi: 2, x_lo: 2; x = x_hi * 2 + x_lo), y: 4, z: 8, core: 2. Of those that a mesh axis runs over, the one named last changes fastest.
Arguments:
- positions: float32 [3, 131072], P(None, ('row', 'col')), may hold values from -6 to 6
- velocities: float32 [3, 131072], P(None, ('row', 'col')), may hold values from -3 to 3
- accel: float32 [3, 131072], P(None, ('row', 'col')), may hold values from -2 to 2
- jerks: float32 [3, 131072], P(None, ('row', 'col')), may hold values from -2 to 2
- act_slot: int32 [2, 16384], P(None, ('row', 'col')), may hold values from 0 to 511, as said below
- act_count: int32 [2, 256], P(None, ('row', 'col')), may hold values from 16 to 64, as said below
Outputs:
- new_positions: float32 [3, 131072], P(None, ('row', 'col'))
- new_velocities: float32 [3, 131072], P(None, ('row', 'col'))
- new_accel: float32 [3, 131072], P(None, ('row', 'col'))
- new_jerks: float32 [3, 131072], P(None, ('row', 'col'))
The draws below stay inside these ranges and needn't reach their ends.
Inputs may be any that keep to these rules, and one draw needn't show every extreme that they name: `act_slot`: within one step the 64 entries of one device are distinct star numbers of that device. `act_count`: some device has all 64 slots live in every step.
All inputs are finite; a program needn't handle non-finite values.
Results may differ from the reference program's by a relative error of at most 0.0001.
Values sent between devices are 32-bit elements; how exact they have to be, the bound alone decides.
No kernel may reach another device: no remote copies, remote signals or barrier semaphores. Data moves between devices by JAX's collectives and lax.ppermute only.
A program may use at most 64 MiB of HBM per device.

```python
import math
import jax
import jax.numpy as jnp
from jax import lax

NS = 512
ACT = 64
STEPS = 2
NSTAR = 131072
NACT = 16384


def draw_act_slot(key, part):
    key = jax.random.fold_in(key, 11)
    owners = NACT // ACT
    subkeys = jax.random.split(key, STEPS * owners)
    chosen = jax.vmap(lambda subkey: jax.random.permutation(subkey, NS)[:ACT])(subkeys)
    return chosen.reshape(STEPS, NACT).astype(jnp.int32)


def draw_act_count(key, part):
    key = jax.random.fold_in(key, 12)
    owners = NACT // ACT
    first, second = jax.random.split(key)
    counts = jax.random.randint(first, (STEPS, owners), ACT // 4, ACT + 1)
    busiest = jax.random.randint(second, (STEPS,), 0, owners)
    counts = jnp.where(jnp.arange(owners)[None, :] == busiest[:, None], ACT, counts)
    return counts.astype(jnp.int32)


def shard_levels(stream_key, extent, pieces, least, high):
    def one(dim, blocks):
        steps = jax.random.uniform(jax.random.fold_in(jax.random.fold_in(stream_key, 6), dim), (blocks,), jnp.float32, least / len(pieces), high / len(pieces))
        return jnp.repeat(jnp.exp(steps), extent[dim] // blocks).reshape((-1,) + (1,) * (len(extent) - dim - 1))

    gain = one(*pieces[0])
    for cut in pieces[1:]:
        gain = gain * one(*cut)
    return gain


def noise(stream_key, dims, deviation, limit, cuts=(), held_as=jnp.bfloat16):
    gain = shard_levels(stream_key, dims, cuts, -0.22, 0.18) if cuts else 1.0
    entries = jax.random.normal(stream_key, dims, jnp.float32) * deviation * gain
    return jnp.minimum(jnp.maximum(entries, -limit), limit).astype(held_as)


def setup_inputs(seed: int = 0) -> dict:
    splits = jax.random.split(jax.random.key(seed), 7)
    positions = noise(splits[0], (3, NSTAR), 1.0, 6.0, ((1, 256),), jnp.float32)
    velocities = noise(splits[1], (3, NSTAR), 0.5, 3.0, ((1, 256),), jnp.float32)
    accel = noise(splits[2], (3, NSTAR), 0.3, 2.0, ((1, 256),), jnp.float32)
    jerks = noise(splits[3], (3, NSTAR), 0.3, 2.0, ((1, 256),), jnp.float32)
    act_slot = draw_act_slot(jax.random.fold_in(splits[6], 71), 0)
    act_count = draw_act_count(jax.random.fold_in(splits[6], 71), 0)
    return dict(positions=positions, velocities=velocities, accel=accel, jerks=jerks, act_slot=act_slot, act_count=act_count)


soften_sq = 0.01
base_step = 1.0 / 64.0

def pair_terms(target_pos, target_vel, source_pos, source_vel):
    offset = source_pos[:, None, :] - target_pos[:, :, None]
    relative = source_vel[:, None, :] - target_vel[:, :, None]
    inv_sq = 1.0 / (lax.optimization_barrier(jnp.sum(offset * offset, 0)) + soften_sq)
    inv_cube = inv_sq * jnp.sqrt(inv_sq)
    radial = 3.0 * lax.optimization_barrier(jnp.sum(offset * relative, 0)) * inv_sq
    accel_sum = lax.optimization_barrier(jnp.sum(inv_cube * offset, -1))
    jerk_sum = lax.optimization_barrier(jnp.sum(inv_cube * (relative - radial * offset), -1))
    return jnp.concatenate([accel_sum, jerk_sum], 0)

def all_forces(active_pos, active_vel, star_pos, star_vel):
    total = active_pos.shape[1]
    nstar = star_pos.shape[1]
    iblock = math.gcd(total, 512)
    jblock = math.gcd(nstar, 4096)
    star_tiles = (star_pos.reshape(3, nstar // jblock, jblock).transpose(1, 0, 2), star_vel.reshape(3, nstar // jblock, jblock).transpose(1, 0, 2))

    def one_block(pair):
        tpos, tvel = pair

        def add_tile(carry, tile):
            return (carry + pair_terms(tpos, tvel, tile[0], tile[1]), None)
        result, unused = lax.scan(add_tile, jnp.zeros((6, iblock), jnp.float32), star_tiles)
        return result
    blocks = (active_pos.reshape(3, total // iblock, iblock).transpose(1, 0, 2), active_vel.reshape(3, total // iblock, iblock).transpose(1, 0, 2))
    result = lax.map(one_block, blocks)
    return result.transpose(1, 0, 2).reshape(6, total) * (1.0 / nstar)

def correct(pred_pos, pred_vel, old_acc, old_jerk, new_acc, new_jerk, stepsize):
    change = old_acc - new_acc
    snap = (-6.0 * change - stepsize * (4.0 * old_jerk + 2.0 * new_jerk)) / (stepsize * stepsize)
    crackle = (12.0 * change + 6.0 * stepsize * (old_jerk + new_jerk)) / (stepsize * stepsize * stepsize)
    fourth = stepsize ** 4 / 24.0
    new_pos = pred_pos + fourth * snap + stepsize ** 5 / 120.0 * crackle
    new_vel = pred_vel + stepsize ** 3 / 6.0 * snap + fourth * crackle
    return (new_pos, new_vel)

def reference(positions, velocities, accel, jerks, act_slot, act_count):
    nstar = positions.shape[1]
    times = jnp.zeros((nstar,), jnp.float32)
    owner = (jnp.arange(NACT) // ACT).astype(jnp.int32) * NS
    for section in range(STEPS):
        now = (section + 1) * base_step
        delta = now - times
        pred_pos = positions + delta * (velocities + delta * (0.5 * accel + delta * jerks / 6.0))
        pred_vel = velocities + delta * (accel + 0.5 * delta * jerks)
        index = (act_slot[section] + owner).astype(jnp.int32)
        live = jnp.arange(NACT) % ACT < jnp.repeat(act_count[section], ACT)
        active_pos = pred_pos[:, index]
        active_vel = pred_vel[:, index]
        forces = all_forces(active_pos, active_vel, pred_pos, pred_vel)
        new_acc = forces[:3]
        new_jerk = forces[3:]
        old_acc = accel[:, index]
        old_jerk = jerks[:, index]
        new_pos, new_vel = correct(active_pos, active_vel, old_acc, old_jerk, new_acc, new_jerk, delta[index])
        positions = positions.at[:, index].set(jnp.where(live, new_pos, positions[:, index]))
        velocities = velocities.at[:, index].set(jnp.where(live, new_vel, velocities[:, index]))
        accel = accel.at[:, index].set(jnp.where(live, new_acc, old_acc))
        jerks = jerks.at[:, index].set(jnp.where(live, new_jerk, old_jerk))
        times = times.at[index].set(jnp.where(live, now, times[index]))
    return (positions, velocities, accel, jerks)
```

```python
import functools

import jax
import jax.numpy as jnp
from jax import lax
from jax.experimental import pallas as pl
from jax.experimental.pallas import tpu as pltpu
from jax.sharding import PartitionSpec as P

STEPS = 2
F32 = jnp.float32
BF16 = jnp.bfloat16

soften_sq = 0.01
base_step = 1.0 / 64.0
grid_step = 1.0 / 32.0

SRC_TILE = 512
TGT_TILE = 512
LANES = 128
WIDE = 80
VMEM_BYTES = 40 << 20


def rounded(x):
    return x.astype(BF16).astype(F32)


def split3(x):
    high = rounded(x)
    rest = x - high
    mid = rounded(rest)
    return high, mid, rounded(rest - mid)


def rows(*pieces):
    return jnp.concatenate(pieces, 0)


def exact_dot(values, picks, dims):
    dot = lambda piece: lax.dot_general(piece.astype(BF16), picks, (dims, ((), ())), preferred_element_type=F32)
    high, mid, low = split3(values)
    return dot(high) + dot(mid) + dot(low)


def pieces(state):
    grid = jnp.round(state * (1.0 / grid_step)) * grid_step
    fine = state - grid
    fine_high = rounded(fine)
    fine_low = rounded(fine - fine_high)
    pos, vel = slice(0, 3), slice(3, 6)
    add = lambda z: z[0:1] + z[1:2] + z[2:3]
    square = add(grid[pos] * grid[pos])
    square_rest = add((2.0 * grid[pos] + fine[pos]) * fine[pos])
    cross = add(grid[pos] * grid[vel])
    cross_rest = add(grid[pos] * fine[vel] + fine[pos] * grid[vel] + fine[pos] * fine[vel])
    return grid, fine_high, fine_low, square, square_rest, cross, cross_rest


def source_table(state):
    grid, high, low, square, square_rest, cross, cross_rest = pieces(state)
    count = state.shape[1]
    one, zero = jnp.ones((1, count), F32), jnp.zeros((1, count), F32)
    b_grid = rows(grid[0:6], one, zero)
    b_square = rows(*split3(square), *split3(cross), one, one)
    b_high = rows(high[0:6], one, one)
    b_low = rows(low[0:6], one, zero)
    b_rest = rows(*split3(square_rest), *split3(cross_rest), zero, zero)
    return rows(b_grid, b_square, b_high, b_low, b_grid, b_grid, b_high, b_low, b_high, b_rest)


def target_tables(state):
    grid, high, low, square, square_rest, cross, cross_rest = pieces(state)
    count = state.shape[1]
    one, zero = jnp.ones((1, count), F32), jnp.zeros((1, count), F32)
    zero2, zero3 = jnp.zeros((2, count), F32), jnp.zeros((3, count), F32)

    def table(factor, units, main, rest):
        m, r = split3(main), split3(rest)
        fg, fh, fl = factor(grid), factor(high), factor(low)
        return rows(
            fg, m[0], zero, *units, m[1], m[2], fg, r[0], r[1], fg, r[2], zero,
            fh, zero2, fl, zero2, fh, zero2, fh, zero2, fl, zero2, *units, zero2,
        )

    distance = table(lambda c: rows(-2.0 * c[0:3], zero3), (one, one, one, zero3), square, square_rest + soften_sq)
    product = table(lambda c: rows(-c[3:6], -c[0:3]), (zero3, one, one, one), cross, cross_rest)
    return distance, product


def dot(a, b):
    return jnp.dot(a, b, preferred_element_type=F32)


def pair_kernel(src_ref, tgt_ref, out_ref, tgt, table, table_t, distance, product):
    blocks, _, per = src_ref.shape
    groups = tgt_ref.shape[0]
    n_src, n_tgt = blocks * per, groups * LANES // 2

    def prepare(i, unused):
        cols = pl.ds(pl.multiple_of(i * per, per), per)
        rows_of = source_table(src_ref[i])
        table[:, cols] = rows_of[:32].astype(BF16)
        table_t[cols, :] = rows_of.T.astype(BF16)
        return unused

    lax.fori_loop(0, blocks, prepare, 0)
    low_half = lax.broadcasted_iota(jnp.int32, (8, LANES), 1) < LANES // 2
    for k in range(groups // 2):
        tgt[:, k * LANES : (k + 1) * LANES] = jnp.where(low_half, tgt_ref[2 * k], tgt_ref[2 * k + 1])
    dist, prod = target_tables(tgt[...])
    distance[...] = dist.astype(BF16)
    product[...] = prod.astype(BF16)

    for t in range(n_tgt // TGT_TILE):
        cols = slice(t * TGT_TILE, (t + 1) * TGT_TILE)

        def source_tile(i, sums):
            here = pl.ds(pl.multiple_of(i * SRC_TILE, SRC_TILE), SRC_TILE)
            left, right = table_t[here, :], table[:, here]
            softened = dot(left, distance[:, cols])
            radial = dot(left, product[:, cols])
            root = lax.rsqrt(softened)
            inv_sq = root * root
            cube = inv_sq * root
            tidal = (radial * inv_sq) * cube
            cube_high, tidal_high = cube.astype(BF16), tidal.astype(BF16)
            cube_low = (cube - cube_high.astype(F32)).astype(BF16)
            tidal_low = (tidal - tidal_high.astype(F32)).astype(BF16)
            return (
                sums[0] + dot(right, cube_high) + dot(right, cube_low),
                sums[1] + dot(right, tidal_high) + dot(right, tidal_low),
            )

        zero = jnp.zeros((32, TGT_TILE), F32)
        cubes, tidals = lax.fori_loop(0, n_src // SRC_TILE, source_tile, (zero, zero))
        here = tgt[:, cols]
        about = lambda sums: sums[0:8] + sums[16:24] + sums[24:32] - here * sums[6:7]
        force, tide = about(cubes), about(tidals)
        result = rows(force[0:3], force[3:6] - 3.0 * tide[0:3], force[6:8])
        for k in range(TGT_TILE // LANES):
            chunk = result[:, k * LANES : (k + 1) * LANES]
            place = 2 * (t * (TGT_TILE // LANES) + k)
            out_ref[place] = chunk
            out_ref[place + 1] = chunk


def pair_sums(sources, targets):
    blocks, _, per = sources.shape
    groups = targets.shape[0]
    n_src, n_tgt = blocks * per, groups * LANES // 2
    pairs = n_src * n_tgt
    return pl.pallas_call(
        pair_kernel,
        out_shape=jax.ShapeDtypeStruct((groups, 8, LANES), F32),
        in_specs=[pl.BlockSpec(memory_space=pltpu.VMEM)] * 2,
        out_specs=pl.BlockSpec(memory_space=pltpu.VMEM),
        scratch_shapes=[
            pltpu.VMEM((8, n_tgt), F32),
            pltpu.VMEM((32, n_src), BF16),
            pltpu.VMEM((n_src, WIDE), BF16),
            pltpu.VMEM((WIDE, n_tgt), BF16),
            pltpu.VMEM((WIDE, n_tgt), BF16),
        ],
        compiler_params=pltpu.CompilerParams(vmem_limit_bytes=VMEM_BYTES),
        cost_estimate=pl.CostEstimate(flops=600 * pairs, bytes_accessed=32 * (n_src + n_tgt), transcendentals=pairs),
        name="pair_sums",
    )(sources, targets)


def predict(pos, vel, acc, jerk, delta):
    new_pos = pos + delta * (vel + delta * (0.5 * acc + delta * jerk / 6.0))
    return new_pos, vel + delta * (acc + 0.5 * delta * jerk)


def correct(pos, vel, old_acc, old_jerk, acc, jerk, step):
    change = old_acc - acc
    snap = (-6.0 * change - step * (4.0 * old_jerk + 2.0 * jerk)) / (step * step)
    crackle = (12.0 * change + 6.0 * step * (old_jerk + jerk)) / (step * step * step)
    square = step * step
    fourth = square * square / 24.0
    new_pos = pos + fourth * snap + square * square * step / 120.0 * crackle
    return new_pos, vel + square * step / 6.0 * snap + fourth * crackle


def picked(slot_ref, section, stars):
    slots = slot_ref[section : section + 1, :]
    twice = jnp.concatenate([slots, slots], 1)
    return (lax.broadcasted_iota(jnp.int32, (stars, LANES), 0) == twice).astype(F32).astype(BF16)


def stage(section, pos, vel, acc, jerk, delta, slot_ref, src_ref, tgt_ref, own_ref):
    stars = pos.shape[1]
    new_pos, new_vel = predict(pos, vel, acc, jerk, delta)
    zero2 = jnp.zeros((2, stars), F32)
    state = rows(new_pos, new_vel, zero2)
    held = rows(acc, jerk, delta, zero2[0:1])
    own = exact_dot(rows(state, held), picked(slot_ref, section, stars), ((1,), (0,)))
    own_ref[...] = own
    for k in range(src_ref.shape[0]):
        src_ref[k] = state
    for k in range(tgt_ref.shape[0]):
        tgt_ref[k] = own[0:8]


def finish(section, row, parts_ref, own_ref, count_ref, slot_ref, state, inv_mass):
    pos, vel, acc, jerk = state
    stars = pos.shape[1]
    total = parts_ref[0]
    for k in range(1, parts_ref.shape[0]):
        total = total + parts_ref[k]
    forces = total * inv_mass
    new_acc, new_jerk = forces[0:3], forces[3:6]
    own = own_ref[...]
    new_pos, new_vel = correct(own[0:3], own[3:6], own[8:11], own[11:14], new_acc, new_jerk, own[14:15])
    lane = lax.broadcasted_iota(jnp.int32, (1, LANES), 1)
    half = LANES // 2
    slot = lane & (half - 1)
    first = row * half
    live = (slot < count_ref[section : section + 1, :]) & (lane >= first) & (lane < first + half)
    fresh = rows(new_pos, new_vel, new_acc, new_jerk, jnp.ones((1, LANES), F32), jnp.zeros((3, LANES), F32))
    fresh = jnp.where(live, fresh, 0.0)
    placed = exact_dot(fresh, picked(slot_ref, section, stars), ((1,), (1,)))
    moved = placed[12:13] > 0.5
    keep = lambda old, k: jnp.where(moved, placed[k : k + 3], old)
    return (keep(pos, 0), keep(vel, 3), keep(acc, 6), keep(jerk, 9)), moved


def first_kernel(pos, vel, acc, jerk, slot_ref, src_ref, tgt_ref, own_ref):
    delta = jnp.full((1, pos.shape[1]), base_step, F32)
    stage(0, pos[...], vel[...], acc[...], jerk[...], delta, slot_ref, src_ref, tgt_ref, own_ref)


def middle_kernel(
    inv_mass, row_ref, pos, vel, acc, jerk, slot_ref, count_ref, parts_ref, own_ref,
    new_pos, new_vel, new_acc, new_jerk, src_ref, tgt_ref, next_ref,
):
    state = (pos[...], vel[...], acc[...], jerk[...])
    state, moved = finish(0, row_ref[0], parts_ref, own_ref, count_ref, slot_ref, state, inv_mass)
    for ref, value in zip((new_pos, new_vel, new_acc, new_jerk), state):
        ref[...] = value
    delta = jnp.where(moved, base_step, 2.0 * base_step)
    stage(1, *state, delta, slot_ref, src_ref, tgt_ref, next_ref)


def last_kernel(
    inv_mass, row_ref, pos, vel, acc, jerk, slot_ref, count_ref, parts_ref, own_ref,
    new_pos, new_vel, new_acc, new_jerk,
):
    state = (pos[...], vel[...], acc[...], jerk[...])
    state, _ = finish(1, row_ref[0], parts_ref, own_ref, count_ref, slot_ref, state, inv_mass)
    for ref, value in zip((new_pos, new_vel, new_acc, new_jerk), state):
        ref[...] = value


def local_call(kernel, outs, operands, scalars=0, name=None):
    vmem = pl.BlockSpec(memory_space=pltpu.VMEM)
    smem = pl.BlockSpec(memory_space=pltpu.SMEM)
    return pl.pallas_call(
        kernel,
        out_shape=[jax.ShapeDtypeStruct(shape, F32) for shape in outs],
        in_specs=[smem] * scalars + [vmem] * (len(operands) - scalars),
        out_specs=[vmem] * len(outs),
        compiler_params=pltpu.CompilerParams(vmem_limit_bytes=VMEM_BYTES),
        name=name,
    )(*operands)


def shards(positions, velocities, accel, jerks, act_slot, act_count):
    stars = positions.shape[1]
    n_row, n_col = lax.axis_size("row"), lax.axis_size("col")
    inv_mass = 1.0 / (stars * n_row * n_col)
    parity = (lax.axis_index("row") % 2).astype(jnp.int32).reshape(1)
    state = (positions, velocities, accel, jerks)
    like = [(3, stars)] * 4
    staged = [(n_col, 8, stars), (n_row, 8, LANES), (16, LANES)]

    def exchanged(src, tgt):
        targets = lax.all_to_all(tgt, "row", 0, 0)
        sources = lax.all_to_all(src, "col", 0, 0)
        return lax.all_to_all(pair_sums(sources, targets), "row", 0, 0)

    src, tgt, own = local_call(first_kernel, staged, (*state, act_slot), name="first")
    parts = exchanged(src, tgt)
    *state, src, tgt, later = local_call(
        functools.partial(middle_kernel, inv_mass), like + staged,
        (parity, *state, act_slot, act_count, parts, own), 1, name="middle",
    )
    parts = exchanged(src, tgt)
    return tuple(
        local_call(
            functools.partial(last_kernel, inv_mass), like,
            (parity, *state, act_slot, act_count, parts, later), 1, name="last",
        )
    )


def solution(mesh):
    placed = P(None, ("row", "col"))
    return jax.shard_map(shards, mesh=mesh, in_specs=(placed,) * 6, out_specs=(placed,) * 4, check_vma=False)
```

```python
import functools

import jax
import jax.numpy as jnp
from jax import lax
from jax.experimental import pallas as pl
from jax.experimental.pallas import tpu as pltpu
from jax.sharding import PartitionSpec as P

STEPS = 2
F32 = jnp.float32
BF16 = jnp.bfloat16

soften_sq = 0.01
base_step = 1.0 / 64.0
grid_step = 1.0 / 32.0

SRC_TILE = 1024
TGT_TILE = 256
UNROLL = 1
LANES = 128
WIDE = 80
VMEM_BYTES = 40 << 20


def rounded(x):
    return x.astype(BF16).astype(F32)


def split3(x):
    high = rounded(x)
    rest = x - high
    mid = rounded(rest)
    return high, mid, rounded(rest - mid)


def rows(*pieces):
    return jnp.concatenate(pieces, 0)


def exact_dot(values, picks, dims):
    count = values.shape[0]
    stacked = rows(*split3(values)).astype(BF16)
    got = lax.dot_general(stacked, picks, (dims, ((), ())), preferred_element_type=F32)
    return got[:count] + got[count : 2 * count] + got[2 * count :]


def pieces(state):
    grid = jnp.round(state * (1.0 / grid_step)) * grid_step
    fine = state - grid
    fine_high = rounded(fine)
    fine_low = rounded(fine - fine_high)
    pos, vel = slice(0, 3), slice(3, 6)
    add = lambda z: z[0:1] + z[1:2] + z[2:3]
    square = add(grid[pos] * grid[pos])
    square_rest = add((2.0 * grid[pos] + fine[pos]) * fine[pos])
    cross = add(grid[pos] * grid[vel])
    cross_rest = add(grid[pos] * fine[vel] + fine[pos] * grid[vel] + fine[pos] * fine[vel])
    return grid, fine_high, fine_low, square, square_rest, cross, cross_rest


def source_table(state):
    grid, high, low, square, square_rest, cross, cross_rest = pieces(state)
    count = state.shape[1]
    one, zero = jnp.ones((1, count), F32), jnp.zeros((1, count), F32)
    b_grid = rows(grid[0:6], one, zero)
    b_square = rows(*split3(square), *split3(cross), one, one)
    b_high = rows(high[0:6], one, one)
    b_low = rows(low[0:6], one, zero)
    b_rest = rows(*split3(square_rest), *split3(cross_rest), zero, zero)
    return rows(b_grid, b_square, b_high, b_low, b_grid, b_grid, b_high, b_low, b_high, b_rest)


def target_tables(state):
    grid, high, low, square, square_rest, cross, cross_rest = pieces(state)
    count = state.shape[1]
    one, zero = jnp.ones((1, count), F32), jnp.zeros((1, count), F32)
    zero2, zero3 = jnp.zeros((2, count), F32), jnp.zeros((3, count), F32)

    def table(factor, units, main, rest):
        m, r = split3(main), split3(rest)
        fg, fh, fl = factor(grid), factor(high), factor(low)
        return rows(
            fg, m[0], zero, *units, m[1], m[2], fg, r[0], r[1], fg, r[2], zero,
            fh, zero2, fl, zero2, fh, zero2, fh, zero2, fl, zero2, *units, zero2,
        )

    distance = table(lambda c: rows(-2.0 * c[0:3], zero3), (one, one, one, zero3), square, square_rest + soften_sq)
    product = table(lambda c: rows(-c[3:6], -c[0:3]), (zero3, one, one, one), cross, cross_rest)
    return distance, product


def dot(a, b):
    return jnp.dot(a, b, preferred_element_type=F32)


def tile_sums(table, table_t, targets, n_src):
    distance, product = target_tables(targets)
    distance, product = distance.astype(BF16), product.astype(BF16)

    def source_tile(i, sums):
        here = pl.ds(pl.multiple_of(i * SRC_TILE, SRC_TILE), SRC_TILE)
        left, right = table_t[here, :], table[:, here]
        softened = dot(left, distance)
        radial = dot(left, product)
        root = lax.rsqrt(softened)
        inv_sq = root * root
        cube = inv_sq * root
        tidal = (radial * inv_sq) * cube
        cube_high, tidal_high = cube.astype(BF16), tidal.astype(BF16)
        cube_low = (cube - cube_high.astype(F32)).astype(BF16)
        tidal_low = (tidal - tidal_high.astype(F32)).astype(BF16)
        return (
            sums[0] + dot(right, cube_high) + dot(right, cube_low),
            sums[1] + dot(right, tidal_high) + dot(right, tidal_low),
        )

    zero = jnp.zeros((32, targets.shape[1]), F32)
    cubes, tidals = lax.fori_loop(0, n_src // SRC_TILE, source_tile, (zero, zero), unroll=UNROLL)
    about = lambda sums: sums[0:8] + sums[16:24] + sums[24:32] - targets * sums[6:7]
    force, tide = about(cubes), about(tidals)
    return rows(force[0:3], force[3:6] - 3.0 * tide[0:3], force[6:8])


def pair_kernel(src_ref, tgt_ref, out_ref, table, table_t, total):
    blocks, _, per = src_ref.shape
    groups = tgt_ref.shape[0]
    half = LANES // 2
    n_src, n_tgt = blocks * per, groups * half

    def prepare(i, unused):
        cols = pl.ds(pl.multiple_of(i * per, per), per)
        rows_of = source_table(src_ref[i])
        table[:, cols] = rows_of[:32].astype(BF16)
        table_t[cols, :] = rows_of.T.astype(BF16)
        return unused

    lax.fori_loop(0, blocks, prepare, 0)
    low_half = lax.broadcasted_iota(jnp.int32, (8, LANES), 1) < half
    targets = jnp.concatenate(
        [jnp.where(low_half, tgt_ref[2 * k], tgt_ref[2 * k + 1]) for k in range(groups // 2)], 1
    )
    lane = lax.broadcasted_iota(jnp.int32, (1, n_tgt), 1)
    slot = (lane & (half - 1)).astype(F32)
    offset = jnp.zeros((1, n_tgt), F32)
    live_count = jnp.zeros((1, 1), F32)
    for k in range(groups):
        count = tgt_ref[k, 6:7, 0:1]
        offset = offset + jnp.where(lane >= (k + 1) * half, count, 0.0)
        live_count = live_count + count
    place = jnp.where(slot < targets[6:7], offset + slot, -1.0).astype(jnp.int32)
    tiles = (jnp.max(live_count).astype(jnp.int32) + (TGT_TILE - 1)) // TGT_TILE
    total[...] = jnp.zeros_like(total)

    def target_tile(t, unused):
        spot = lax.broadcasted_iota(jnp.int32, (TGT_TILE, n_tgt), 0) + t * TGT_TILE
        pack = (spot == place).astype(F32).astype(BF16)
        sums = tile_sums(table, table_t, exact_dot(targets, pack, ((1,), (1,))), n_src)
        total[...] += exact_dot(sums, pack, ((1,), (0,)))
        return unused

    lax.fori_loop(0, tiles, target_tile, 0)
    for k in range(groups // 2):
        chunk = total[:, k * LANES : (k + 1) * LANES]
        out_ref[2 * k] = chunk
        out_ref[2 * k + 1] = chunk


def pair_sums(sources, targets):
    blocks, _, per = sources.shape
    groups = targets.shape[0]
    n_src, n_tgt = blocks * per, groups * LANES // 2
    pairs = n_src * n_tgt
    return pl.pallas_call(
        pair_kernel,
        out_shape=jax.ShapeDtypeStruct((groups, 8, LANES), F32),
        in_specs=[pl.BlockSpec(memory_space=pltpu.VMEM)] * 2,
        out_specs=pl.BlockSpec(memory_space=pltpu.VMEM),
        scratch_shapes=[
            pltpu.VMEM((32, n_src), BF16),
            pltpu.VMEM((n_src, WIDE), BF16),
            pltpu.VMEM((8, n_tgt), F32),
        ],
        compiler_params=pltpu.CompilerParams(vmem_limit_bytes=VMEM_BYTES),
        cost_estimate=pl.CostEstimate(flops=600 * pairs, bytes_accessed=32 * (n_src + n_tgt), transcendentals=pairs),
        name="pair_sums",
    )(sources, targets)


def predict(pos, vel, acc, jerk, delta):
    new_pos = pos + delta * (vel + delta * (0.5 * acc + delta * jerk / 6.0))
    return new_pos, vel + delta * (acc + 0.5 * delta * jerk)


def correct(pos, vel, old_acc, old_jerk, acc, jerk, step):
    change = old_acc - acc
    snap = (-6.0 * change - step * (4.0 * old_jerk + 2.0 * jerk)) / (step * step)
    crackle = (12.0 * change + 6.0 * step * (old_jerk + jerk)) / (step * step * step)
    square = step * step
    fourth = square * square / 24.0
    new_pos = pos + fourth * snap + square * square * step / 120.0 * crackle
    return new_pos, vel + square * step / 6.0 * snap + fourth * crackle


def picked(slot_ref, section, stars):
    slots = slot_ref[section : section + 1, :]
    twice = jnp.concatenate([slots, slots], 1)
    return (lax.broadcasted_iota(jnp.int32, (stars, LANES), 0) == twice).astype(F32).astype(BF16)


def stage(section, pos, vel, acc, jerk, delta, slot_ref, count_ref, src_ref, tgt_ref, own_ref):
    stars = pos.shape[1]
    new_pos, new_vel = predict(pos, vel, acc, jerk, delta)
    zero2 = jnp.zeros((2, stars), F32)
    state = rows(new_pos, new_vel, zero2)
    held = rows(acc, jerk, delta, zero2[0:1])
    own = exact_dot(rows(state, held), picked(slot_ref, section, stars), ((1,), (0,)))
    own_ref[...] = own
    count = jnp.broadcast_to(count_ref[section : section + 1, :].astype(F32), (1, LANES))
    target = rows(own[0:6], count, jnp.zeros((1, LANES), F32))
    for k in range(src_ref.shape[0]):
        src_ref[k] = state
    for k in range(tgt_ref.shape[0]):
        tgt_ref[k] = target


def finish(section, side, parts_ref, own_ref, count_ref, slot_ref, state, inv_mass):
    pos, vel, acc, jerk = state
    stars = pos.shape[1]
    total = parts_ref[0]
    for k in range(1, parts_ref.shape[0]):
        total = total + parts_ref[k]
    forces = total * inv_mass
    new_acc, new_jerk = forces[0:3], forces[3:6]
    own = own_ref[...]
    new_pos, new_vel = correct(own[0:3], own[3:6], own[8:11], own[11:14], new_acc, new_jerk, own[14:15])
    lane = lax.broadcasted_iota(jnp.int32, (1, LANES), 1)
    half = LANES // 2
    slot = lane & (half - 1)
    first = side * half
    live = (slot < count_ref[section : section + 1, :]) & (lane >= first) & (lane < first + half)
    fresh = rows(new_pos, new_vel, new_acc, new_jerk, jnp.ones((1, LANES), F32), jnp.zeros((3, LANES), F32))
    fresh = jnp.where(live, fresh, 0.0)
    placed = exact_dot(fresh, picked(slot_ref, section, stars), ((1,), (1,)))
    moved = placed[12:13] > 0.5
    keep = lambda old, k: jnp.where(moved, placed[k : k + 3], old)
    return (keep(pos, 0), keep(vel, 3), keep(acc, 6), keep(jerk, 9)), moved


def first_kernel(*refs):
    arrays, (src_ref, tgt_ref, own_ref), held, sems = refs[:6], refs[6:9], refs[9:15], refs[15]
    copies = [pltpu.make_async_copy(a, b, sems.at[k]) for k, (a, b) in enumerate(zip(arrays, held))]
    for copy in copies:
        copy.start()
    for copy in copies:
        copy.wait()
    pos, vel, acc, jerk, slot_ref, count_ref = held
    delta = jnp.full((1, pos.shape[1]), base_step, F32)
    stage(0, pos[...], vel[...], acc[...], jerk[...], delta, slot_ref, count_ref, src_ref, tgt_ref, own_ref)


def middle_kernel(
    inv_mass, side_ref, pos, vel, acc, jerk, slot_ref, count_ref, parts_ref, own_ref,
    new_pos, new_vel, new_acc, new_jerk, src_ref, tgt_ref, next_ref,
):
    state = (pos[...], vel[...], acc[...], jerk[...])
    state, moved = finish(0, side_ref[0], parts_ref, own_ref, count_ref, slot_ref, state, inv_mass)
    for ref, value in zip((new_pos, new_vel, new_acc, new_jerk), state):
        ref[...] = value
    delta = jnp.where(moved, base_step, 2.0 * base_step)
    stage(1, *state, delta, slot_ref, count_ref, src_ref, tgt_ref, next_ref)


def last_kernel(
    inv_mass, side_ref, pos, vel, acc, jerk, slot_ref, count_ref, parts_ref, own_ref,
    new_pos, new_vel, new_acc, new_jerk,
):
    state = (pos[...], vel[...], acc[...], jerk[...])
    state, _ = finish(1, side_ref[0], parts_ref, own_ref, count_ref, slot_ref, state, inv_mass)
    for ref, value in zip((new_pos, new_vel, new_acc, new_jerk), state):
        ref[...] = value


def local_call(kernel, outs, operands, places, scratch=(), name=None):
    spec = lambda place: pl.BlockSpec(memory_space=place)
    return pl.pallas_call(
        kernel,
        out_shape=[jax.ShapeDtypeStruct(shape, F32) for shape in outs],
        in_specs=[spec(place) for place in places],
        out_specs=[spec(pltpu.VMEM)] * len(outs),
        scratch_shapes=list(scratch),
        compiler_params=pltpu.CompilerParams(vmem_limit_bytes=VMEM_BYTES),
        name=name,
    )(*operands)


def shards(positions, velocities, accel, jerks, act_slot, act_count):
    stars = positions.shape[1]
    n_row, n_col = lax.axis_size("row"), lax.axis_size("col")
    inv_mass = 1.0 / (stars * n_row * n_col)
    side = (lax.axis_index("col") % 2).astype(jnp.int32).reshape(1)
    state = (positions, velocities, accel, jerks)
    like = [(3, stars)] * 4
    staged = [(n_row, 8, stars), (n_col, 8, LANES), (16, LANES)]
    inside = [pltpu.SMEM] + [pltpu.VMEM] * 8

    def exchanged(src, tgt):
        targets = lax.all_to_all(tgt, "col", 0, 0)
        sources = lax.all_to_all(src, "row", 0, 0)
        return lax.all_to_all(pair_sums(sources, targets), "col", 0, 0)

    everything = (*state, act_slot, act_count)
    held = [pltpu.VMEM(x.shape, x.dtype) for x in everything] + [pltpu.SemaphoreType.DMA((6,))]
    src, tgt, own = local_call(first_kernel, staged, everything, [pl.ANY] * 6, held, name="first")
    parts = exchanged(src, tgt)
    *state, src, tgt, later = local_call(
        functools.partial(middle_kernel, inv_mass), like + staged,
        (side, *state, act_slot, act_count, parts, own), inside, name="middle",
    )
    parts = exchanged(src, tgt)
    return tuple(
        local_call(
            functools.partial(last_kernel, inv_mass), like,
            (side, *state, act_slot, act_count, parts, later), inside, name="last",
        )
    )


def solution(mesh):
    placed = P(None, ("row", "col"))
    return jax.shard_map(shards, mesh=mesh, in_specs=(placed,) * 6, out_specs=(placed,) * 4, check_vma=False)
```

```python
import functools

import jax
import jax.numpy as jnp
from jax import lax
from jax.experimental import pallas as pl
from jax.experimental.pallas import tpu as pltpu
from jax.sharding import PartitionSpec as P

STEPS = 2
F32 = jnp.float32
BF16 = jnp.bfloat16

soften_sq = 0.01
base_step = 1.0 / 64.0
grid_step = 1.0 / 32.0

SRC_TILE = 1024
TGT_TILE = 256
LANES = 128
WIDE = 80
VMEM_BYTES = 40 << 20


def rounded(x):
    return x.astype(BF16).astype(F32)


def split3(x):
    high = rounded(x)
    rest = x - high
    mid = rounded(rest)
    return high, mid, rounded(rest - mid)


def rows(*pieces):
    return jnp.concatenate(pieces, 0)


def exact_dot(values, picks, dims):
    count = values.shape[0]
    stacked = rows(*split3(values)).astype(BF16)
    got = lax.dot_general(stacked, picks, (dims, ((), ())), preferred_element_type=F32)
    return got[:count] + got[count : 2 * count] + got[2 * count :]


def pieces(state):
    grid = jnp.round(state * (1.0 / grid_step)) * grid_step
    fine = state - grid
    fine_high = rounded(fine)
    fine_low = rounded(fine - fine_high)
    pos, vel = slice(0, 3), slice(3, 6)
    add = lambda z: z[0:1] + z[1:2] + z[2:3]
    square = add(grid[pos] * grid[pos])
    square_rest = add((2.0 * grid[pos] + fine[pos]) * fine[pos])
    cross = add(grid[pos] * grid[vel])
    cross_rest = add(grid[pos] * fine[vel] + fine[pos] * grid[vel] + fine[pos] * fine[vel])
    return grid, fine_high, fine_low, square, square_rest, cross, cross_rest


def source_tables(state):
    grid, high, low, square, square_rest, cross, cross_rest = pieces(state)
    count = state.shape[1]
    one, zero = jnp.ones((1, count), F32), jnp.zeros((1, count), F32)
    zero6, zero8 = jnp.zeros((6, count), F32), jnp.zeros((8, count), F32)
    b_grid = rows(grid[0:6], one, zero)
    b_square = rows(*split3(square), *split3(cross), one, one)
    b_high = rows(high[0:6], one, one)
    b_low = rows(low[0:6], one, zero)
    b_rest = rows(*split3(square_rest), *split3(cross_rest), zero, zero)
    pair = rows(b_grid, b_square, b_high, b_low, b_grid, b_grid, b_high, b_low, b_high, b_rest)
    force = rows(b_grid, b_high, b_low, zero8)
    tide = rows(grid[0:3], high[0:3], low[0:3], one, zero6)
    return pair.astype(BF16), force.astype(BF16), tide.astype(BF16)


def target_tables(state):
    grid, high, low, square, square_rest, cross, cross_rest = pieces(state)
    count = state.shape[1]
    one, zero = jnp.ones((1, count), F32), jnp.zeros((1, count), F32)
    zero2, zero3 = jnp.zeros((2, count), F32), jnp.zeros((3, count), F32)

    def table(factor, units, main, rest):
        m, r = split3(main), split3(rest)
        fg, fh, fl = factor(grid), factor(high), factor(low)
        return rows(
            fg, m[0], zero, *units, m[1], m[2], fg, r[0], r[1], fg, r[2], zero,
            fh, zero2, fl, zero2, fh, zero2, fh, zero2, fl, zero2, *units, zero2,
        )

    distance = table(lambda c: rows(-2.0 * c[0:3], zero3), (one, one, one, zero3), square, square_rest + soften_sq)
    product = table(lambda c: rows(-c[3:6], -c[0:3]), (zero3, one, one, one), cross, cross_rest)
    return distance, product


def dot(a, b):
    return jnp.dot(a, b, preferred_element_type=F32)


def tile_sums(tables, targets, n_src, prepare=None):
    pair, force, tide = tables
    distance, product = target_tables(targets)
    distance, product = distance.astype(BF16), product.astype(BF16)
    last = n_src // SRC_TILE - 1

    def source_tile(i, sums):
        here = pl.ds(pl.multiple_of(i * SRC_TILE, SRC_TILE), SRC_TILE)
        left, right, right_tide = pair[here, :], force[:, here], tide[:, here]
        softened = dot(left, distance)
        radial = dot(left, product)
        root = lax.rsqrt(softened)
        inv_sq = root * root
        cube = inv_sq * root
        tidal = (radial * inv_sq) * cube
        cube_high, tidal_high = cube.astype(BF16), tidal.astype(BF16)
        cube_low = (cube - cube_high.astype(F32)).astype(BF16)
        tidal_low = (tidal - tidal_high.astype(F32)).astype(BF16)
        sums = (
            sums[0] + dot(right, cube_high) + dot(right, cube_low),
            sums[1] + dot(right_tide, tidal_high) + dot(right_tide, tidal_low),
        )
        if prepare is not None:
            prepare(jnp.minimum(i + 1, last))
        return sums

    if prepare is not None:
        prepare(0)
    zero = lambda count: jnp.zeros((count, targets.shape[1]), F32)
    forces, tides = lax.fori_loop(0, last + 1, source_tile, (zero(32), zero(16)))
    pulls = forces[0:8] + forces[8:16] + forces[16:24] - targets * forces[6:7]
    turns = (tides[0:3] + tides[3:6] + tides[6:9]) - targets[0:3] * tides[9:10]
    return rows(pulls[0:3], pulls[3:6] - 3.0 * turns, pulls[6:8])


def pair_kernel(src_ref, tgt_ref, out_ref, pair, force, tide, total):
    blocks, per = src_ref.shape[0], src_ref.shape[1] // 6 * LANES
    groups = tgt_ref.shape[0]
    half = LANES // 2
    n_src, n_tgt = blocks * per, groups * half

    def prepare(i):
        for k in range(SRC_TILE // per):
            block = i * (SRC_TILE // per) + k
            cols = pl.ds(pl.multiple_of(block * per, per), per)
            packed = src_ref[block]
            state = jnp.concatenate([packed[6 * c : 6 * c + 6] for c in range(per // LANES)], 1)
            pair_rows, force[:, cols], tide[:, cols] = source_tables(state)
            pair[cols, :] = pair_rows.T

    low_half = lax.broadcasted_iota(jnp.int32, (8, LANES), 1) < half
    targets = jnp.concatenate(
        [jnp.where(low_half, tgt_ref[2 * k], tgt_ref[2 * k + 1]) for k in range(groups // 2)], 1
    )
    lane = lax.broadcasted_iota(jnp.int32, (1, n_tgt), 1)
    slot = (lane & (half - 1)).astype(F32)
    offset = jnp.zeros((1, n_tgt), F32)
    live_count = jnp.zeros((1, 1), F32)
    for k in range(groups):
        count = tgt_ref[k, 6:7, 0:1]
        offset = offset + jnp.where(lane >= (k + 1) * half, count, 0.0)
        live_count = live_count + count
    place = jnp.where(slot < targets[6:7], offset + slot, -1.0).astype(jnp.int32)
    tiles = (jnp.max(live_count).astype(jnp.int32) + (TGT_TILE - 1)) // TGT_TILE
    total[...] = jnp.zeros_like(total)

    def target_tile(t, unused, make=None):
        spot = lax.broadcasted_iota(jnp.int32, (TGT_TILE, n_tgt), 0) + t * TGT_TILE
        pack = (spot == place).astype(F32).astype(BF16)
        sums = tile_sums((pair, force, tide), exact_dot(targets, pack, ((1,), (1,))), n_src, make)
        total[...] += exact_dot(sums, pack, ((1,), (0,)))
        return unused

    target_tile(0, 0, prepare)
    lax.fori_loop(1, tiles, target_tile, 0)
    for k in range(groups // 2):
        chunk = total[:, k * LANES : (k + 1) * LANES]
        out_ref[2 * k] = chunk
        out_ref[2 * k + 1] = chunk


def pair_sums(sources, targets):
    blocks, per = sources.shape[0], sources.shape[1] // 6 * LANES
    groups = targets.shape[0]
    n_src, n_tgt = blocks * per, groups * LANES // 2
    pairs = n_src * n_tgt
    return pl.pallas_call(
        pair_kernel,
        out_shape=jax.ShapeDtypeStruct((groups, 8, LANES), F32),
        in_specs=[pl.BlockSpec(memory_space=pltpu.VMEM)] * 2,
        out_specs=pl.BlockSpec(memory_space=pltpu.VMEM),
        scratch_shapes=[
            pltpu.VMEM((n_src, WIDE), BF16),
            pltpu.VMEM((32, n_src), BF16),
            pltpu.VMEM((16, n_src), BF16),
            pltpu.VMEM((8, n_tgt), F32),
        ],
        compiler_params=pltpu.CompilerParams(vmem_limit_bytes=VMEM_BYTES),
        cost_estimate=pl.CostEstimate(flops=600 * pairs, bytes_accessed=32 * (n_src + n_tgt), transcendentals=pairs),
        name="pair_sums",
    )(sources, targets)


def predict(pos, vel, acc, jerk, delta):
    new_pos = pos + delta * (vel + delta * (0.5 * acc + delta * jerk / 6.0))
    return new_pos, vel + delta * (acc + 0.5 * delta * jerk)


def correct(pos, vel, old_acc, old_jerk, acc, jerk, step):
    change = old_acc - acc
    snap = (-6.0 * change - step * (4.0 * old_jerk + 2.0 * jerk)) / (step * step)
    crackle = (12.0 * change + 6.0 * step * (old_jerk + jerk)) / (step * step * step)
    square = step * step
    fourth = square * square / 24.0
    new_pos = pos + fourth * snap + square * square * step / 120.0 * crackle
    return new_pos, vel + square * step / 6.0 * snap + fourth * crackle


def picked(slot_ref, section, stars):
    slots = slot_ref[section : section + 1, :]
    twice = jnp.concatenate([slots, slots], 1)
    return (lax.broadcasted_iota(jnp.int32, (stars, LANES), 0) == twice).astype(F32).astype(BF16)


def stage(section, pos, vel, acc, jerk, delta, slot_ref, count_ref, src_ref, tgt_ref, own_ref):
    stars = pos.shape[1]
    new_pos, new_vel = predict(pos, vel, acc, jerk, delta)
    zero2 = jnp.zeros((2, stars), F32)
    state = rows(new_pos, new_vel, zero2)
    packed = rows(*(state[0:6, k : k + LANES] for k in range(0, stars, LANES)))
    held = rows(acc, jerk, delta, zero2[0:1])
    own = exact_dot(rows(state, held), picked(slot_ref, section, stars), ((1,), (0,)))
    own_ref[...] = own
    count = jnp.full((1, LANES), count_ref[section], jnp.int32).astype(F32)
    target = rows(own[0:6], count, jnp.zeros((1, LANES), F32))
    for k in range(src_ref.shape[0]):
        src_ref[k] = packed
    for k in range(tgt_ref.shape[0]):
        tgt_ref[k] = target


def finish(section, side, parts_ref, own_ref, count_ref, slot_ref, state, inv_mass):
    pos, vel, acc, jerk = state
    stars = pos.shape[1]
    total = parts_ref[0]
    for k in range(1, parts_ref.shape[0]):
        total = total + parts_ref[k]
    forces = total * inv_mass
    new_acc, new_jerk = forces[0:3], forces[3:6]
    own = own_ref[...]
    new_pos, new_vel = correct(own[0:3], own[3:6], own[8:11], own[11:14], new_acc, new_jerk, own[14:15])
    lane = lax.broadcasted_iota(jnp.int32, (1, LANES), 1)
    half = LANES // 2
    slot = lane & (half - 1)
    first = side * half
    live = (slot < count_ref[section]) & (lane >= first) & (lane < first + half)
    fresh = rows(new_pos, new_vel, new_acc, new_jerk, jnp.ones((1, LANES), F32), jnp.zeros((3, LANES), F32))
    fresh = jnp.where(live, fresh, 0.0)
    placed = exact_dot(fresh, picked(slot_ref, section, stars), ((1,), (1,)))
    moved = placed[12:13] > 0.5
    keep = lambda old, k: jnp.where(moved, placed[k : k + 3], old)
    return (keep(pos, 0), keep(vel, 3), keep(acc, 6), keep(jerk, 9)), moved


def first_kernel(*refs):
    count_ref, arrays, (src_ref, tgt_ref, own_ref), held, sems = refs[0], refs[1:6], refs[6:9], refs[9:14], refs[14]
    copies = [pltpu.make_async_copy(a, b, sems.at[k]) for k, (a, b) in enumerate(zip(arrays, held))]
    for copy in copies:
        copy.start()
    for copy in copies:
        copy.wait()
    pos, vel, acc, jerk, slot_ref = held
    delta = jnp.full((1, pos.shape[1]), base_step, F32)
    stage(0, pos[...], vel[...], acc[...], jerk[...], delta, slot_ref, count_ref, src_ref, tgt_ref, own_ref)


def middle_kernel(
    inv_mass, side_ref, count_ref, pos, vel, acc, jerk, slot_ref, parts_ref, own_ref,
    new_pos, new_vel, new_acc, new_jerk, src_ref, tgt_ref, next_ref,
):
    state = (pos[...], vel[...], acc[...], jerk[...])
    state, moved = finish(0, side_ref[0], parts_ref, own_ref, count_ref, slot_ref, state, inv_mass)
    for ref, value in zip((new_pos, new_vel, new_acc, new_jerk), state):
        ref[...] = value
    delta = jnp.where(moved, base_step, 2.0 * base_step)
    stage(1, *state, delta, slot_ref, count_ref, src_ref, tgt_ref, next_ref)


def last_kernel(
    inv_mass, side_ref, count_ref, pos, vel, acc, jerk, slot_ref, parts_ref, own_ref,
    new_pos, new_vel, new_acc, new_jerk,
):
    state = (pos[...], vel[...], acc[...], jerk[...])
    state, _ = finish(1, side_ref[0], parts_ref, own_ref, count_ref, slot_ref, state, inv_mass)
    for ref, value in zip((new_pos, new_vel, new_acc, new_jerk), state):
        ref[...] = value


def local_call(kernel, outs, operands, places, scratch=(), vmem=VMEM_BYTES, name=None):
    spec = lambda place: pl.BlockSpec(memory_space=place)
    return pl.pallas_call(
        kernel,
        out_shape=[jax.ShapeDtypeStruct(shape, F32) for shape in outs],
        in_specs=[spec(place) for place in places],
        out_specs=[spec(pltpu.VMEM)] * len(outs),
        scratch_shapes=list(scratch),
        compiler_params=pltpu.CompilerParams(vmem_limit_bytes=vmem),
        name=name,
    )(*operands)


def shards(positions, velocities, accel, jerks, act_slot, act_count):
    stars = positions.shape[1]
    n_row, n_col = lax.axis_size("row"), lax.axis_size("col")
    inv_mass = 1.0 / (stars * n_row * n_col)
    side = (lax.axis_index("col") % 2).astype(jnp.int32).reshape(1)
    state = (positions, velocities, accel, jerks)
    like = [(3, stars)] * 4
    staged = [(n_row, 6 * stars // LANES, LANES), (n_col, 8, LANES), (16, LANES)]
    inside = [pltpu.SMEM] * 2 + [pltpu.VMEM] * 7
    counts = act_count.reshape(-1)

    def exchanged(src, tgt):
        targets = lax.all_to_all(tgt, "col", 0, 0)
        sources = lax.all_to_all(src, "row", 0, 0)
        return lax.all_to_all(pair_sums(sources, targets), "col", 0, 0)

    everything = (*state, act_slot)
    held = [pltpu.VMEM(x.shape, x.dtype) for x in everything] + [pltpu.SemaphoreType.DMA((5,))]
    src, tgt, own = local_call(first_kernel, staged, (counts, *everything), [pltpu.SMEM] + [pl.ANY] * 5, held, None, name="first")
    parts = exchanged(src, tgt)
    *state, src, tgt, later = local_call(
        functools.partial(middle_kernel, inv_mass), like + staged,
        (side, counts, *state, act_slot, parts, own), inside, name="middle",
    )
    parts = exchanged(src, tgt)
    return tuple(
        local_call(
            functools.partial(last_kernel, inv_mass), like,
            (side, counts, *state, act_slot, parts, later), inside, name="last",
        )
    )


def solution(mesh):
    placed = P(None, ("row", "col"))
    return jax.shard_map(shards, mesh=mesh, in_specs=(placed,) * 6, out_specs=(placed,) * 4, check_vma=False)
```

```python
import functools

import jax
import jax.numpy as jnp
from jax import lax
from jax.experimental import pallas as pl
from jax.experimental.pallas import tpu as pltpu
from jax.sharding import PartitionSpec as P

F32 = jnp.float32
BF16 = jnp.bfloat16

soften_sq = 0.01
base_step = 1.0 / 64.0
grid_step = 1.0 / 32.0

SRC_TILE = 1024
TGT_TILE = 256
LANES = 128
WIDE = 80
VMEM_BYTES = 40 << 20


def rounded(x):
    return x.astype(BF16).astype(F32)


def split3(x):
    high = rounded(x)
    rest = x - high
    mid = rounded(rest)
    return high, mid, rounded(rest - mid)


def rows(*pieces):
    return jnp.concatenate(pieces, 0)


def exact_dot(values, picks, dims):
    count = values.shape[0]
    stacked = rows(*split3(values)).astype(BF16)
    got = lax.dot_general(stacked, picks, (dims, ((), ())), preferred_element_type=F32)
    return got[:count] + got[count : 2 * count] + got[2 * count :]


def pieces(state):
    grid = jnp.round(state * (1.0 / grid_step)) * grid_step
    fine = state - grid
    fine_high = rounded(fine)
    fine_low = rounded(fine - fine_high)
    pos, vel = slice(0, 3), slice(3, 6)
    add = lambda z: z[0:1] + z[1:2] + z[2:3]
    square = add(grid[pos] * grid[pos])
    square_rest = add((2.0 * grid[pos] + fine[pos]) * fine[pos])
    cross = add(grid[pos] * grid[vel])
    cross_rest = add(grid[pos] * fine[vel] + fine[pos] * grid[vel] + fine[pos] * fine[vel])
    return grid, fine_high, fine_low, square, square_rest, cross, cross_rest


def source_tables(state):
    grid, high, low, square, square_rest, cross, cross_rest = pieces(state)
    count = state.shape[1]
    one, zero = jnp.ones((1, count), F32), jnp.zeros((1, count), F32)
    zero6, zero8 = jnp.zeros((6, count), F32), jnp.zeros((8, count), F32)
    b_grid = rows(grid[0:6], one, zero)
    b_square = rows(*split3(square), *split3(cross), one, one)
    b_high = rows(high[0:6], one, one)
    b_low = rows(low[0:6], one, zero)
    b_rest = rows(*split3(square_rest), *split3(cross_rest), zero, zero)
    pair = rows(b_grid, b_square, b_high, b_low, b_grid, b_grid, b_high, b_low, b_high, b_rest)
    force = rows(b_grid, b_high, b_low, zero8)
    tide = rows(grid[0:3], high[0:3], low[0:3], one, zero6)
    return pair.astype(BF16), force.astype(BF16), tide.astype(BF16)


def target_tables(state):
    grid, high, low, square, square_rest, cross, cross_rest = pieces(state)
    count = state.shape[1]
    one, zero = jnp.ones((1, count), F32), jnp.zeros((1, count), F32)
    zero2, zero3 = jnp.zeros((2, count), F32), jnp.zeros((3, count), F32)

    def table(factor, units, main, rest):
        m, r = split3(main), split3(rest)
        fg, fh, fl = factor(grid), factor(high), factor(low)
        return rows(
            fg, m[0], zero, *units, m[1], m[2], fg, r[0], r[1], fg, r[2], zero,
            fh, zero2, fl, zero2, fh, zero2, fh, zero2, fl, zero2, *units, zero2,
        )

    distance = table(lambda c: rows(-2.0 * c[0:3], zero3), (one, one, one, zero3), square, square_rest + soften_sq)
    product = table(lambda c: rows(-c[3:6], -c[0:3]), (zero3, one, one, one), cross, cross_rest)
    return distance, product


def dot(a, b):
    return jnp.dot(a, b, preferred_element_type=F32)


def tile_sums(tables, targets, n_src, prepare=None):
    pair, force, tide = tables
    distance, product = target_tables(targets)
    distance, product = distance.astype(BF16), product.astype(BF16)
    last = n_src // SRC_TILE - 1

    def source_tile(i, sums):
        here = pl.ds(pl.multiple_of(i * SRC_TILE, SRC_TILE), SRC_TILE)
        left, right, right_tide = pair[here, :], force[:, here], tide[:, here]
        softened = dot(left, distance)
        radial = dot(left, product)
        root = lax.rsqrt(softened)
        inv_sq = root * root
        cube = inv_sq * root
        tidal = (radial * inv_sq) * cube
        cube_high, tidal_high = cube.astype(BF16), tidal.astype(BF16)
        cube_low = (cube - cube_high.astype(F32)).astype(BF16)
        tidal_low = (tidal - tidal_high.astype(F32)).astype(BF16)
        sums = (
            sums[0] + dot(right, cube_high) + dot(right, cube_low),
            sums[1] + dot(right_tide, tidal_high) + dot(right_tide, tidal_low),
        )
        if prepare is not None:
            prepare(jnp.minimum(i + 1, last))
        return sums

    if prepare is not None:
        prepare(0)
    zero = lambda count: jnp.zeros((count, targets.shape[1]), F32)
    forces, tides = lax.fori_loop(0, last + 1, source_tile, (zero(32), zero(16)))
    pulls = forces[0:8] + forces[8:16] + forces[16:24] - targets * forces[6:7]
    turns = (tides[0:3] + tides[3:6] + tides[6:9]) - targets[0:3] * tides[9:10]
    return rows(pulls[0:3], pulls[3:6] - 3.0 * turns, pulls[6:8])


def unpacked(ref, section):
    half = LANES // 2
    lower = lax.broadcasted_iota(jnp.int32, ref.shape[1:], 1) < half
    halves = []
    for k in range(ref.shape[0] // 2):
        even, odd = ref[2 * k], ref[2 * k + 1]
        if section == 0:
            odd = pltpu.roll(odd, half, 1)
        else:
            even = pltpu.roll(even, half, 1)
        halves.append(jnp.where(lower, even, odd))
    return jnp.concatenate(halves, 1)


def pair_kernel(gathered, src_ref, tgt_ref, out_ref, pair, force, tide, total):
    blocks, per = src_ref.shape[0], src_ref.shape[1] // 6 * LANES
    half = LANES // 2
    if gathered:
        info = unpacked(tgt_ref, 0)
        targets = rows(info[0:6], info[12:13], info[15:16])
    else:
        targets = tgt_ref[...]
    n_src, n_tgt = blocks * per, targets.shape[1]

    def prepare(i):
        for k in range(SRC_TILE // per):
            block = i * (SRC_TILE // per) + k
            cols = pl.ds(pl.multiple_of(block * per, per), per)
            packed = src_ref[block]
            state = jnp.concatenate([packed[6 * c : 6 * c + 6] for c in range(per // LANES)], 1)
            pair_rows, force[:, cols], tide[:, cols] = source_tables(state)
            pair[cols, :] = pair_rows.T

    lane = lax.broadcasted_iota(jnp.int32, (1, n_tgt), 1)
    slot = (lane & (half - 1)).astype(F32)
    offset = jnp.zeros((1, n_tgt), F32)
    live_count = jnp.zeros((1, 1), F32)
    for k in range(n_tgt // half):
        count = targets[6:7, k * half : k * half + 1]
        offset = offset + jnp.where(lane >= (k + 1) * half, count, 0.0)
        live_count = live_count + count
    place = jnp.where(slot < targets[6:7], offset + slot, -1.0).astype(jnp.int32)
    tiles = (jnp.max(live_count).astype(jnp.int32) + (TGT_TILE - 1)) // TGT_TILE
    total[...] = jnp.zeros_like(total)

    def target_tile(t, unused, make=None):
        spot = lax.broadcasted_iota(jnp.int32, (TGT_TILE, n_tgt), 0) + t * TGT_TILE
        pack = (spot == place).astype(F32).astype(BF16)
        sums = tile_sums((pair, force, tide), exact_dot(targets, pack, ((1,), (1,))), n_src, make)
        total[...] += exact_dot(sums, pack, ((1,), (0,)))
        return unused

    target_tile(0, 0, prepare)
    lax.fori_loop(1, tiles, target_tile, 0)
    if gathered:
        whole = rows(*(total[0:6, k : k + LANES] for k in range(0, n_tgt, LANES)))
        for k in range(out_ref.shape[0]):
            out_ref[k] = whole
    else:
        for k in range(out_ref.shape[0]):
            out_ref[k] = total[:, k // 2 * LANES : (k // 2 + 1) * LANES]


def pair_sums(sources, targets, n_col):
    gathered = targets.ndim == 3
    n_src, n_tgt = sources.shape[0] * sources.shape[1] // 6 * LANES, n_col * LANES // 2
    pairs = n_src * n_tgt
    return pl.pallas_call(
        functools.partial(pair_kernel, gathered),
        out_shape=jax.ShapeDtypeStruct((n_col, 6 * n_tgt // LANES if gathered else 8, LANES), F32),
        in_specs=[pl.BlockSpec(memory_space=pltpu.VMEM)] * 2,
        out_specs=pl.BlockSpec(memory_space=pltpu.VMEM),
        scratch_shapes=[
            pltpu.VMEM((n_src, WIDE), BF16),
            pltpu.VMEM((32, n_src), BF16),
            pltpu.VMEM((16, n_src), BF16),
            pltpu.VMEM((8, n_tgt), F32),
        ],
        compiler_params=pltpu.CompilerParams(vmem_limit_bytes=VMEM_BYTES),
        cost_estimate=pl.CostEstimate(flops=600 * pairs, bytes_accessed=32 * (n_src + n_tgt), transcendentals=pairs),
        name="pair_sums",
    )(sources, targets)


def predict(pos, vel, acc, jerk, delta):
    new_pos = pos + delta * (vel + delta * (0.5 * acc + delta * jerk / 6.0))
    return new_pos, vel + delta * (acc + 0.5 * delta * jerk)


def correct(pos, vel, old_acc, old_jerk, acc, jerk, step):
    change = old_acc - acc
    snap = (-6.0 * change - step * (4.0 * old_jerk + 2.0 * jerk)) / (step * step)
    crackle = (12.0 * change + 6.0 * step * (old_jerk + jerk)) / (step * step * step)
    square = step * step
    fourth = square * square / 24.0
    new_pos = pos + fourth * snap + square * square * step / 120.0 * crackle
    return new_pos, vel + square * step / 6.0 * snap + fourth * crackle


def picked(low_slots, high_slots, stars):
    slots = jnp.concatenate([low_slots, high_slots], 1)
    return (lax.broadcasted_iota(jnp.int32, (stars, LANES), 0) == slots).astype(F32).astype(BF16)


def send_sources(pos, vel, src_ref):
    state = rows(pos, vel)
    packed = rows(*(state[:, k : k + LANES] for k in range(0, state.shape[1], LANES)))
    for k in range(src_ref.shape[0]):
        src_ref[k] = packed


def first_kernel(*refs):
    count_ref, arrays, (src_ref, tgt_ref), held, sems = refs[0], refs[1:6], refs[6:8], refs[8:13], refs[13]
    copies = [pltpu.make_async_copy(a, b, sems.at[k]) for k, (a, b) in enumerate(zip(arrays, held))]
    for copy in copies:
        copy.start()
    for copy in copies:
        copy.wait()
    pos, vel, acc, jerk = (ref[...] for ref in held[:4])
    slots = held[4][...]
    now = predict(pos, vel, acc, jerk, base_step)
    later = predict(pos, vel, acc, jerk, 2.0 * base_step)
    send_sources(*now, src_ref)
    lower = lax.broadcasted_iota(jnp.int32, (1, LANES), 1) < LANES // 2
    picks = picked(slots[0:1], slots[1:2], pos.shape[1])
    zero6 = jnp.zeros((6, pos.shape[1]), F32)
    own = exact_dot(rows(*now, *later, acc, jerk, zero6), picks, ((1,), (0,)))
    counts = jnp.where(lower, count_ref[0], count_ref[1]).astype(F32)
    slot = jnp.concatenate([slots[0:1], slots[1:2]], 1).astype(F32)
    target = rows(jnp.where(lower, own[0:6], own[6:12]), own[12:18], counts, slot, own[18:20])
    for k in range(tgt_ref.shape[0]):
        tgt_ref[k] = target


def middle_kernel(
    inv_mass, here_ref, count_ref, pos, vel, acc, jerk, slot_ref, parts_ref, info_ref,
    new_pos, new_vel, new_acc, new_jerk, src_ref, tgt_ref, own_ref,
):
    total = parts_ref[0]
    for k in range(1, parts_ref.shape[0]):
        total = total + parts_ref[k]
    forces = jnp.concatenate([total[k : k + 6] for k in range(0, total.shape[0], 6)], 1) * inv_mass
    active, after = unpacked(info_ref, 0), unpacked(info_ref, 1)
    n_tgt, half, stars = active.shape[1], LANES // 2, pos.shape[1]
    lane = lax.broadcasted_iota(jnp.int32, (1, n_tgt), 1)
    live = (lane & (half - 1)).astype(F32) < active[12:13]
    at_pos, at_vel = correct(active[0:3], active[3:6], active[6:9], active[9:12], forces[0:3], forces[3:6], base_step)
    one, zero3 = jnp.ones((1, n_tgt), F32), jnp.zeros((3, n_tgt), F32)
    fresh = jnp.where(live, rows(at_pos, at_vel, forces, one, zero3), 0.0)

    mine = jnp.where(lane // half == here_ref[0], active[13:14], -1.0).astype(jnp.int32)
    put = (lax.broadcasted_iota(jnp.int32, (stars, n_tgt), 0) == mine).astype(F32).astype(BF16)
    placed = exact_dot(fresh, put, ((1,), (1,)))
    moved = placed[12:13] > 0.5
    keep = lambda old, k: jnp.where(moved, placed[k : k + 3], old[...])
    state = (keep(pos, 0), keep(vel, 3), keep(acc, 6), keep(jerk, 9))
    for ref, value in zip((new_pos, new_vel, new_acc, new_jerk), state):
        ref[...] = value
    delta = jnp.where(moved, base_step, 2.0 * base_step)
    sources = predict(*state, delta)
    send_sources(*sources, src_ref)
    slots = slot_ref[1:2, :]
    zero = jnp.zeros((1, stars), F32)
    own = exact_dot(rows(*sources, *state[2:], delta, zero, zero, zero), picked(slots, slots, stars), ((1,), (0,)))
    own_ref[...] = rows(own[0:13], jnp.full((1, LANES), count_ref[1], jnp.int32).astype(F32), own[13:15])

    moving = predict(fresh[0:3], fresh[3:6], fresh[6:9], fresh[9:12], base_step)
    moving = rows(*moving, fresh[12:14])
    was = jnp.where(live, active[13:14], -1.0) + (lane // half * stars).astype(F32)
    was = jnp.where(live, was, -1.0)
    will = after[13:14] + (lane // half * stars).astype(F32)
    span = 2 * LANES
    for k in range(0, n_tgt, span):
        cols = slice(k, k + span)
        column = jnp.broadcast_to(will[:, cols], (8, span)).T[:, 0:1]
        same = (column == was[:, cols]).astype(F32).astype(BF16)
        got = exact_dot(moving[:, cols], same, ((1,), (1,)))
        state = jnp.where(got[6:7] > 0.5, got[0:6], after[0:6, cols])
        tgt_ref[:, cols] = rows(state, after[12:13, cols], after[15:16, cols])


def last_kernel(
    inv_mass, side_ref, pos, vel, acc, jerk, slot_ref, parts_ref, own_ref,
    new_pos, new_vel, new_acc, new_jerk,
):
    stars, half = pos.shape[1], LANES // 2
    total = parts_ref[0]
    for k in range(1, parts_ref.shape[0]):
        total = total + parts_ref[k]
    forces = total[0:6] * inv_mass
    own = own_ref[...]
    at_pos, at_vel = correct(own[0:3], own[3:6], own[6:9], own[9:12], forces[0:3], forces[3:6], own[12:13])
    lane = lax.broadcasted_iota(jnp.int32, (1, LANES), 1)
    first = (side_ref[0] & 1) * half
    live = ((lane & (half - 1)).astype(F32) < own[13:14]) & (lane >= first) & (lane < first + half)
    fresh = rows(at_pos, at_vel, forces, jnp.ones((1, LANES), F32), jnp.zeros((3, LANES), F32))
    slots = slot_ref[1:2, :]
    placed = exact_dot(jnp.where(live, fresh, 0.0), picked(slots, slots, stars), ((1,), (1,)))
    moved = placed[12:13] > 0.5
    keep = lambda old, k: jnp.where(moved, placed[k : k + 3], old[...])
    new_pos[...], new_vel[...], new_acc[...], new_jerk[...] = keep(pos, 0), keep(vel, 3), keep(acc, 6), keep(jerk, 9)


def local_call(kernel, outs, operands, places, scratch=(), vmem=VMEM_BYTES, name=None):
    spec = lambda place: pl.BlockSpec(memory_space=place)
    return pl.pallas_call(
        kernel,
        out_shape=[jax.ShapeDtypeStruct(shape, F32) for shape in outs],
        in_specs=[spec(place) for place in places],
        out_specs=[spec(pltpu.VMEM)] * len(outs),
        scratch_shapes=list(scratch),
        compiler_params=pltpu.CompilerParams(vmem_limit_bytes=vmem),
        name=name,
    )(*operands)


def shards(positions, velocities, accel, jerks, act_slot, act_count):
    stars = positions.shape[1]
    n_row, n_col = lax.axis_size("row"), lax.axis_size("col")
    inv_mass = 1.0 / (stars * n_row * n_col)
    here = lax.axis_index("col").astype(jnp.int32).reshape(1)
    counts = act_count.reshape(-1)
    state = (positions, velocities, accel, jerks)
    like = [(3, stars)] * 4
    sources = (n_row, 6 * stars // LANES, LANES)

    everything = (*state, act_slot)
    held = [pltpu.VMEM(x.shape, x.dtype) for x in everything] + [pltpu.SemaphoreType.DMA((5,))]
    src, tgt = local_call(
        first_kernel, [sources, (n_col, 16, LANES)], (counts, *everything), [pltpu.SMEM] + [pl.ANY] * 5, held, None, name="first"
    )
    info = lax.all_to_all(tgt, "col", 0, 0)
    src = lax.all_to_all(src, "row", 0, 0)
    parts = lax.all_to_all(pair_sums(src, info, n_col), "col", 0, 0)
    *state, src, tgt, own = local_call(
        functools.partial(middle_kernel, inv_mass), like + [sources, (8, n_col * LANES // 2), (16, LANES)],
        (here, counts, *state, act_slot, parts, info), [pltpu.SMEM] * 2 + [pltpu.VMEM] * 7, name="middle",
    )
    src = lax.all_to_all(src, "row", 0, 0)
    parts = lax.all_to_all(pair_sums(src, tgt, n_col), "col", 0, 0)
    return tuple(
        local_call(
            functools.partial(last_kernel, inv_mass), like,
            (here, *state, act_slot, parts, own), [pltpu.SMEM] + [pltpu.VMEM] * 7, name="last",
        )
    )


def solution(mesh):
    placed = P(None, ("row", "col"))
    return jax.shard_map(shards, mesh=mesh, in_specs=(placed,) * 6, out_specs=(placed,) * 4, check_vma=False)
```

```python
import functools

import jax
import jax.numpy as jnp
from jax import lax
from jax.experimental import pallas as pl
from jax.experimental.pallas import tpu as pltpu
from jax.sharding import PartitionSpec as P

F32 = jnp.float32
BF16 = jnp.bfloat16

soften_sq = 0.01
base_step = 1.0 / 64.0
grid_step = 1.0 / 32.0

SRC_TILE = 1024
TGT_TILE = 256
LANES = 128
WIDE = 80
VMEM_BYTES = 40 << 20
ROUNDS = ((2, 4, 6), (8,), (1,))


def rounded(x):
    return x.astype(BF16).astype(F32)


def split3(x):
    high = rounded(x)
    rest = x - high
    mid = rounded(rest)
    return high, mid, rounded(rest - mid)


def rows(*pieces):
    return jnp.concatenate(pieces, 0)


def exact_dot(values, picks, dims):
    count = values.shape[0]
    stacked = rows(*split3(values)).astype(BF16)
    got = lax.dot_general(stacked, picks, (dims, ((), ())), preferred_element_type=F32)
    return got[:count] + got[count : 2 * count] + got[2 * count :]


def pieces(state):
    grid = jnp.round(state * (1.0 / grid_step)) * grid_step
    fine = state - grid
    fine_high = rounded(fine)
    fine_low = rounded(fine - fine_high)
    pos, vel = slice(0, 3), slice(3, 6)
    add = lambda z: z[0:1] + z[1:2] + z[2:3]
    square = add(grid[pos] * grid[pos])
    square_rest = add((2.0 * grid[pos] + fine[pos]) * fine[pos])
    cross = add(grid[pos] * grid[vel])
    cross_rest = add(grid[pos] * fine[vel] + fine[pos] * grid[vel] + fine[pos] * fine[vel])
    return grid, fine_high, fine_low, square, square_rest, cross, cross_rest


def source_tables(state):
    grid, high, low, square, square_rest, cross, cross_rest = pieces(state)
    count = state.shape[1]
    one, zero = jnp.ones((1, count), F32), jnp.zeros((1, count), F32)
    zero6, zero8 = jnp.zeros((6, count), F32), jnp.zeros((8, count), F32)
    b_grid = rows(grid[0:6], one, zero)
    b_square = rows(*split3(square), *split3(cross), one, one)
    b_high = rows(high[0:6], one, one)
    b_low = rows(low[0:6], one, zero)
    b_rest = rows(*split3(square_rest), *split3(cross_rest), zero, zero)
    pair = rows(b_grid, b_square, b_high, b_low, b_grid, b_grid, b_high, b_low, b_high, b_rest)
    force = rows(b_grid, b_high, b_low, zero8)
    tide = rows(grid[0:3], high[0:3], low[0:3], one, zero6)
    return pair.astype(BF16), force.astype(BF16), tide.astype(BF16)


def target_tables(state):
    grid, high, low, square, square_rest, cross, cross_rest = pieces(state)
    count = state.shape[1]
    one, zero = jnp.ones((1, count), F32), jnp.zeros((1, count), F32)
    zero2, zero3 = jnp.zeros((2, count), F32), jnp.zeros((3, count), F32)

    def table(factor, units, main, rest):
        m, r = split3(main), split3(rest)
        fg, fh, fl = factor(grid), factor(high), factor(low)
        return rows(
            fg, m[0], zero, *units, m[1], m[2], fg, r[0], r[1], fg, r[2], zero,
            fh, zero2, fl, zero2, fh, zero2, fh, zero2, fl, zero2, *units, zero2,
        )

    distance = table(lambda c: rows(-2.0 * c[0:3], zero3), (one, one, one, zero3), square, square_rest + soften_sq)
    product = table(lambda c: rows(-c[3:6], -c[0:3]), (zero3, one, one, one), cross, cross_rest)
    return distance, product


def dot(a, b):
    return jnp.dot(a, b, preferred_element_type=F32)


def tile_sums(tables, targets, n_src, prepare=None):
    pair, force, tide = tables
    distance, product = target_tables(targets)
    distance, product = distance.astype(BF16), product.astype(BF16)
    last = n_src // SRC_TILE - 1

    def source_tile(i, sums):
        here = pl.ds(pl.multiple_of(i * SRC_TILE, SRC_TILE), SRC_TILE)
        left, right, right_tide = pair[here, :], force[:, here], tide[:, here]
        softened = dot(left, distance)
        radial = dot(left, product)
        root = lax.rsqrt(softened)
        inv_sq = root * root
        cube = inv_sq * root
        tidal = (radial * inv_sq) * cube
        cube_high, tidal_high = cube.astype(BF16), tidal.astype(BF16)
        cube_low = (cube - cube_high.astype(F32)).astype(BF16)
        tidal_low = (tidal - tidal_high.astype(F32)).astype(BF16)
        sums = (
            sums[0] + dot(right, cube_high) + dot(right, cube_low),
            sums[1] + dot(right_tide, tidal_high) + dot(right_tide, tidal_low),
        )
        if prepare is not None:
            prepare(jnp.minimum(i + 1, last))
        return sums

    if prepare is not None:
        prepare(0)
    zero = lambda count: jnp.zeros((count, targets.shape[1]), F32)
    forces, tides = lax.fori_loop(0, last + 1, source_tile, (zero(32), zero(16)))
    pulls = forces[0:8] + forces[8:16] + forces[16:24] - targets * forces[6:7]
    turns = (tides[0:3] + tides[3:6] + tides[6:9]) - targets[0:3] * tides[9:10]
    return rows(pulls[0:3], pulls[3:6] - 3.0 * turns, pulls[6:8])


def block_at(k):
    apart = lax.axis_index("col") ^ k
    return ((apart >> 1) & 3) | ((apart >> 1) & 4) | ((apart & 1) << 3)


def unpacked(ref, section):
    half = LANES // 2
    lower = lax.broadcasted_iota(jnp.int32, ref.shape[1:], 1) < half
    halves = []
    for k in range(ref.shape[0] // 2):
        even, odd = ref[block_at(2 * k)], ref[block_at(2 * k + 1)]
        if section == 0:
            odd = pltpu.roll(odd, half, 1)
        else:
            even = pltpu.roll(even, half, 1)
        halves.append(jnp.where(lower, even, odd))
    return jnp.concatenate(halves, 1)


def pair_kernel(gathered, src_ref, tgt_ref, out_ref, pair, force, tide, total):
    blocks, per = src_ref.shape[0], src_ref.shape[1] // 6 * LANES
    half = LANES // 2
    if gathered:
        info = unpacked(tgt_ref, 0)
        targets = rows(info[0:6], info[12:13], info[15:16])
    else:
        targets = tgt_ref[...]
    n_src, n_tgt = blocks * per, targets.shape[1]

    def prepare(i):
        for k in range(SRC_TILE // per):
            block = i * (SRC_TILE // per) + k
            cols = pl.ds(pl.multiple_of(block * per, per), per)
            packed = src_ref[block]
            state = jnp.concatenate([packed[6 * c : 6 * c + 6] for c in range(per // LANES)], 1)
            pair_rows, force[:, cols], tide[:, cols] = source_tables(state)
            pair[cols, :] = pair_rows.T

    lane = lax.broadcasted_iota(jnp.int32, (1, n_tgt), 1)
    slot = (lane & (half - 1)).astype(F32)
    offset = jnp.zeros((1, n_tgt), F32)
    live_count = jnp.zeros((1, 1), F32)
    for k in range(n_tgt // half):
        count = targets[6:7, k * half : k * half + 1]
        offset = offset + jnp.where(lane >= (k + 1) * half, count, 0.0)
        live_count = live_count + count
    place = jnp.where(slot < targets[6:7], offset + slot, -1.0).astype(jnp.int32)
    tiles = (jnp.max(live_count).astype(jnp.int32) + (TGT_TILE - 1)) // TGT_TILE
    total[...] = jnp.zeros_like(total)

    def target_tile(t, unused, make=None):
        spot = lax.broadcasted_iota(jnp.int32, (TGT_TILE, n_tgt), 0) + t * TGT_TILE
        pack = (spot == place).astype(F32).astype(BF16)
        sums = tile_sums((pair, force, tide), exact_dot(targets, pack, ((1,), (1,))), n_src, make)
        total[...] += exact_dot(sums, pack, ((1,), (0,)))
        return unused

    target_tile(0, 0, prepare)
    lax.fori_loop(1, tiles, target_tile, 0)
    if gathered:
        whole = rows(*(total[0:6, k : k + LANES] for k in range(0, n_tgt, LANES)))
        for k in range(out_ref.shape[0]):
            out_ref[k] = whole
    else:
        for k in range(out_ref.shape[0]):
            out_ref[k] = total[:, k // 2 * LANES : (k // 2 + 1) * LANES]


def pair_sums(sources, targets, n_col):
    gathered = targets.ndim == 3
    n_src, n_tgt = sources.shape[0] * sources.shape[1] // 6 * LANES, n_col * LANES // 2
    pairs = n_src * n_tgt
    return pl.pallas_call(
        functools.partial(pair_kernel, gathered),
        out_shape=jax.ShapeDtypeStruct((n_col, 6 * n_tgt // LANES if gathered else 8, LANES), F32),
        in_specs=[pl.BlockSpec(memory_space=pltpu.VMEM)] * 2,
        out_specs=pl.BlockSpec(memory_space=pltpu.VMEM),
        scratch_shapes=[
            pltpu.VMEM((n_src, WIDE), BF16),
            pltpu.VMEM((32, n_src), BF16),
            pltpu.VMEM((16, n_src), BF16),
            pltpu.VMEM((8, n_tgt), F32),
        ],
        compiler_params=pltpu.CompilerParams(vmem_limit_bytes=VMEM_BYTES),
        cost_estimate=pl.CostEstimate(flops=600 * pairs, bytes_accessed=32 * (n_src + n_tgt), transcendentals=pairs),
        name="pair_sums",
    )(sources, targets)


def predict(pos, vel, acc, jerk, delta):
    new_pos = pos + delta * (vel + delta * (0.5 * acc + delta * jerk / 6.0))
    return new_pos, vel + delta * (acc + 0.5 * delta * jerk)


def correct(pos, vel, old_acc, old_jerk, acc, jerk, step):
    change = old_acc - acc
    snap = (-6.0 * change - step * (4.0 * old_jerk + 2.0 * jerk)) / (step * step)
    crackle = (12.0 * change + 6.0 * step * (old_jerk + jerk)) / (step * step * step)
    square = step * step
    fourth = square * square / 24.0
    new_pos = pos + fourth * snap + square * square * step / 120.0 * crackle
    return new_pos, vel + square * step / 6.0 * snap + fourth * crackle


def picked(low_slots, high_slots, stars):
    slots = jnp.concatenate([low_slots, high_slots], 1)
    return (lax.broadcasted_iota(jnp.int32, (stars, LANES), 0) == slots).astype(F32).astype(BF16)


def send_sources(pos, vel, src_ref):
    state = rows(pos, vel)
    packed = rows(*(state[:, k : k + LANES] for k in range(0, state.shape[1], LANES)))
    for k in range(src_ref.shape[0]):
        src_ref[k] = packed


def first_kernel(*refs):
    count_ref, arrays, (src_ref, tgt_ref), held, sems = refs[0], refs[1:6], refs[6:8], refs[8:13], refs[13]
    copies = [pltpu.make_async_copy(a, b, sems.at[k]) for k, (a, b) in enumerate(zip(arrays, held))]
    for copy in copies:
        copy.start()
    for copy in copies:
        copy.wait()
    pos, vel, acc, jerk = (ref[...] for ref in held[:4])
    slots = held[4][...]
    now = predict(pos, vel, acc, jerk, base_step)
    later = predict(pos, vel, acc, jerk, 2.0 * base_step)
    send_sources(*now, src_ref)
    lower = lax.broadcasted_iota(jnp.int32, (1, LANES), 1) < LANES // 2
    picks = picked(slots[0:1], slots[1:2], pos.shape[1])
    zero6 = jnp.zeros((6, pos.shape[1]), F32)
    own = exact_dot(rows(*now, *later, acc, jerk, zero6), picks, ((1,), (0,)))
    counts = jnp.where(lower, count_ref[0], count_ref[1]).astype(F32)
    slot = jnp.concatenate([slots[0:1], slots[1:2]], 1).astype(F32)
    target = rows(jnp.where(lower, own[0:6], own[6:12]), own[12:18], counts, slot, own[18:20])
    tgt_ref[0] = target


def middle_kernel(
    inv_mass, count_ref, pos, vel, acc, jerk, slot_ref, parts_ref, info_ref,
    new_pos, new_vel, new_acc, new_jerk, src_ref, tgt_ref, own_ref,
):
    total = parts_ref[0]
    for k in range(1, parts_ref.shape[0]):
        total = total + parts_ref[k]
    forces = jnp.concatenate([total[k : k + 6] for k in range(0, total.shape[0], 6)], 1) * inv_mass
    active, after = unpacked(info_ref, 0), unpacked(info_ref, 1)
    n_tgt, half, stars = active.shape[1], LANES // 2, pos.shape[1]
    lane = lax.broadcasted_iota(jnp.int32, (1, n_tgt), 1)
    live = (lane & (half - 1)).astype(F32) < active[12:13]
    at_pos, at_vel = correct(active[0:3], active[3:6], active[6:9], active[9:12], forces[0:3], forces[3:6], base_step)
    one, zero3 = jnp.ones((1, n_tgt), F32), jnp.zeros((3, n_tgt), F32)
    fresh = jnp.where(live, rows(at_pos, at_vel, forces, one, zero3), 0.0)

    mine = jnp.where(lane // half == lax.axis_index("col"), active[13:14], -1.0).astype(jnp.int32)
    put = (lax.broadcasted_iota(jnp.int32, (stars, n_tgt), 0) == mine).astype(F32).astype(BF16)
    placed = exact_dot(fresh, put, ((1,), (1,)))
    moved = placed[12:13] > 0.5
    keep = lambda old, k: jnp.where(moved, placed[k : k + 3], old[...])
    state = (keep(pos, 0), keep(vel, 3), keep(acc, 6), keep(jerk, 9))
    for ref, value in zip((new_pos, new_vel, new_acc, new_jerk), state):
        ref[...] = value
    delta = jnp.where(moved, base_step, 2.0 * base_step)
    sources = predict(*state, delta)
    send_sources(*sources, src_ref)
    slots = slot_ref[1:2, :]
    zero = jnp.zeros((1, stars), F32)
    own = exact_dot(rows(*sources, *state[2:], delta, zero, zero, zero), picked(slots, slots, stars), ((1,), (0,)))
    own_ref[...] = rows(own[0:13], jnp.full((1, LANES), count_ref[1], jnp.int32).astype(F32), own[13:15])

    moving = predict(fresh[0:3], fresh[3:6], fresh[6:9], fresh[9:12], base_step)
    moving = rows(*moving, fresh[12:14])
    was = jnp.where(live, active[13:14], -1.0) + (lane // half * stars).astype(F32)
    was = jnp.where(live, was, -1.0)
    will = after[13:14] + (lane // half * stars).astype(F32)
    span = 2 * LANES
    for k in range(0, n_tgt, span):
        cols = slice(k, k + span)
        column = jnp.broadcast_to(will[:, cols], (8, span)).T[:, 0:1]
        same = (column == was[:, cols]).astype(F32).astype(BF16)
        got = exact_dot(moving[:, cols], same, ((1,), (1,)))
        state = jnp.where(got[6:7] > 0.5, got[0:6], after[0:6, cols])
        tgt_ref[:, cols] = rows(state, after[12:13, cols], after[15:16, cols])


def last_kernel(
    inv_mass, pos, vel, acc, jerk, slot_ref, parts_ref, own_ref,
    new_pos, new_vel, new_acc, new_jerk,
):
    stars, half = pos.shape[1], LANES // 2
    total = parts_ref[0]
    for k in range(1, parts_ref.shape[0]):
        total = total + parts_ref[k]
    forces = total[0:6] * inv_mass
    own = own_ref[...]
    at_pos, at_vel = correct(own[0:3], own[3:6], own[6:9], own[9:12], forces[0:3], forces[3:6], own[12:13])
    lane = lax.broadcasted_iota(jnp.int32, (1, LANES), 1)
    first = (lax.axis_index("col") & 1) * half
    live = ((lane & (half - 1)).astype(F32) < own[13:14]) & (lane >= first) & (lane < first + half)
    fresh = rows(at_pos, at_vel, forces, jnp.ones((1, LANES), F32), jnp.zeros((3, LANES), F32))
    slots = slot_ref[1:2, :]
    placed = exact_dot(jnp.where(live, fresh, 0.0), picked(slots, slots, stars), ((1,), (1,)))
    moved = placed[12:13] > 0.5
    keep = lambda old, k: jnp.where(moved, placed[k : k + 3], old[...])
    new_pos[...], new_vel[...], new_acc[...], new_jerk[...] = keep(pos, 0), keep(vel, 3), keep(acc, 6), keep(jerk, 9)


def local_call(kernel, outs, operands, places, scratch=(), vmem=VMEM_BYTES, name=None):
    spec = lambda place: pl.BlockSpec(memory_space=place)
    return pl.pallas_call(
        kernel,
        out_shape=[jax.ShapeDtypeStruct(shape, F32) for shape in outs],
        in_specs=[spec(place) for place in places],
        out_specs=[spec(pltpu.VMEM)] * len(outs),
        scratch_shapes=list(scratch),
        compiler_params=pltpu.CompilerParams(vmem_limit_bytes=vmem),
        name=name,
    )(*operands)


def shards(positions, velocities, accel, jerks, act_slot, act_count):
    stars = positions.shape[1]
    n_row, n_col = lax.axis_size("row"), lax.axis_size("col")
    inv_mass = 1.0 / (stars * n_row * n_col)
    counts = act_count.reshape(-1)
    state = (positions, velocities, accel, jerks)
    like = [(3, stars)] * 4
    sources = (n_row, 6 * stars // LANES, LANES)

    everything = (*state, act_slot)
    held = [pltpu.VMEM(x.shape, x.dtype) for x in everything] + [pltpu.SemaphoreType.DMA((5,))]
    src, tgt = local_call(
        first_kernel, [sources, (1, 16, LANES)], (counts, *everything), [pltpu.SMEM] + [pl.ANY] * 5, held, None, name="first"
    )
    src = lax.all_to_all(src, "row", 0, 0)
    info = tgt
    for masks in ROUNDS:
        others = [lax.ppermute(info, "col", [(k, k ^ mask) for k in range(n_col)]) for mask in masks]
        info = jnp.concatenate([info, *others])
    parts = lax.all_to_all(pair_sums(src, info, n_col), "col", 0, 0)
    *state, src, tgt, own = local_call(
        functools.partial(middle_kernel, inv_mass), like + [sources, (8, n_col * LANES // 2), (16, LANES)],
        (counts, *state, act_slot, parts, info), [pltpu.SMEM] + [pltpu.VMEM] * 7, name="middle",
    )
    src = lax.all_to_all(src, "row", 0, 0)
    parts = lax.all_to_all(pair_sums(src, tgt, n_col), "col", 0, 0)
    return tuple(
        local_call(
            functools.partial(last_kernel, inv_mass), like,
            (*state, act_slot, parts, own), [pltpu.VMEM] * 7, name="last",
        )
    )


def solution(mesh):
    placed = P(None, ("row", "col"))
    return jax.shard_map(shards, mesh=mesh, in_specs=(placed,) * 6, out_specs=(placed,) * 4, check_vma=False)
```

```python
import functools

import jax
import jax.numpy as jnp
from jax import lax
from jax.experimental import pallas as pl
from jax.experimental.pallas import tpu as pltpu
from jax.sharding import PartitionSpec as P

F32 = jnp.float32
BF16 = jnp.bfloat16

soften_sq = 0.01
base_step = 1.0 / 64.0
grid_step = 1.0 / 32.0

SRC_TILE = 4096
SRC_STEP = 256
TGT_TILE = 256
LANES = 128
WIDE = 80
VMEM_BYTES = 40 << 20
ROUNDS = ((2, 4, 6), (8,), (1,))


def rounded(x):
    return x.astype(BF16).astype(F32)


def split3(x):
    high = rounded(x)
    rest = x - high
    mid = rounded(rest)
    return high, mid, rounded(rest - mid)


def rows(*pieces):
    return jnp.concatenate(pieces, 0)


def exact_dot(values, picks, dims):
    count = values.shape[0]
    stacked = rows(*split3(values)).astype(BF16)
    got = lax.dot_general(stacked, picks, (dims, ((), ())), preferred_element_type=F32)
    return got[:count] + got[count : 2 * count] + got[2 * count :]


def pieces(state):
    grid = jnp.round(state * (1.0 / grid_step)) * grid_step
    fine = state - grid
    fine_high = rounded(fine)
    fine_low = rounded(fine - fine_high)
    pos, vel = slice(0, 3), slice(3, 6)
    add = lambda z: z[0:1] + z[1:2] + z[2:3]
    square = add(grid[pos] * grid[pos])
    square_rest = add((2.0 * grid[pos] + fine[pos]) * fine[pos])
    cross = add(grid[pos] * grid[vel])
    cross_rest = add(grid[pos] * fine[vel] + fine[pos] * grid[vel] + fine[pos] * fine[vel])
    return grid, fine_high, fine_low, square, square_rest, cross, cross_rest


def source_tables(state):
    grid, high, low, square, square_rest, cross, cross_rest = pieces(state)
    count = state.shape[1]
    one, zero = jnp.ones((1, count), F32), jnp.zeros((1, count), F32)
    zero6, zero8 = jnp.zeros((6, count), F32), jnp.zeros((8, count), F32)
    b_grid = rows(grid[0:6], one, zero)
    b_square = rows(*split3(square), *split3(cross), one, one)
    b_high = rows(high[0:6], one, one)
    b_low = rows(low[0:6], one, zero)
    b_rest = rows(*split3(square_rest), *split3(cross_rest), zero, zero)
    pair = rows(b_grid, b_square, b_high, b_low, b_grid, b_grid, b_high, b_low, b_high, b_rest)
    force = rows(b_grid, b_high, b_low, zero8)
    tide = rows(grid[0:3], high[0:3], low[0:3], one, zero6)
    return pair.astype(BF16), force.astype(BF16), tide.astype(BF16)


def target_tables(state):
    grid, high, low, square, square_rest, cross, cross_rest = pieces(state)
    count = state.shape[1]
    one, zero = jnp.ones((1, count), F32), jnp.zeros((1, count), F32)
    zero2, zero3 = jnp.zeros((2, count), F32), jnp.zeros((3, count), F32)

    def table(factor, units, main, rest):
        m, r = split3(main), split3(rest)
        fg, fh, fl = factor(grid), factor(high), factor(low)
        return rows(
            fg, m[0], zero, *units, m[1], m[2], fg, r[0], r[1], fg, r[2], zero,
            fh, zero2, fl, zero2, fh, zero2, fh, zero2, fl, zero2, *units, zero2,
        )

    distance = table(lambda c: rows(-2.0 * c[0:3], zero3), (one, one, one, zero3), square, square_rest + soften_sq)
    product = table(lambda c: rows(-c[3:6], -c[0:3]), (zero3, one, one, one), cross, cross_rest)
    return distance, product


def dot(a, b):
    return jnp.dot(a, b, preferred_element_type=F32)


def tile_sums(tables, targets, n_src, prepare=None):
    pair, force, tide = tables
    distance, product = target_tables(targets)
    distance, product = distance.astype(BF16), product.astype(BF16)
    last = n_src // SRC_TILE - 1

    def products(i, k):
        here = pl.ds(pl.multiple_of(i * SRC_TILE + k * SRC_STEP, SRC_STEP), SRC_STEP)
        left = pair[here, :]
        return dot(left, distance), dot(left, product)

    def collected(i, k, softened, radial, sums):
        here = pl.ds(pl.multiple_of(i * SRC_TILE + k * SRC_STEP, SRC_STEP), SRC_STEP)
        right, right_tide = force[:, here], tide[:, here]
        root = lax.rsqrt(softened)
        inv_sq = root * root
        cube = inv_sq * root
        tidal = (radial * inv_sq) * cube
        cube_high, tidal_high = cube.astype(BF16), tidal.astype(BF16)
        cube_low = (cube - cube_high.astype(F32)).astype(BF16)
        tidal_low = (tidal - tidal_high.astype(F32)).astype(BF16)
        return (
            sums[0] + dot(right, cube_high) + dot(right, cube_low),
            sums[1] + dot(right_tide, tidal_high) + dot(right_tide, tidal_low),
        )

    def source_tile(i, sums):
        steps = SRC_TILE // SRC_STEP
        ahead = products(i, 0)
        for k in range(steps):
            now = ahead
            if k + 1 < steps:
                ahead = products(i, k + 1)
            sums = collected(i, k, *now, sums)
        if prepare is not None:
            prepare(jnp.minimum(i + 1, last))
        return sums

    if prepare is not None:
        prepare(0)
    zero = lambda count: jnp.zeros((count, targets.shape[1]), F32)
    forces, tides = lax.fori_loop(0, last + 1, source_tile, (zero(32), zero(16)))
    pulls = forces[0:8] + forces[8:16] + forces[16:24] - targets * forces[6:7]
    turns = (tides[0:3] + tides[3:6] + tides[6:9]) - targets[0:3] * tides[9:10]
    return rows(pulls[0:3], pulls[3:6] - 3.0 * turns, pulls[6:8])


def block_at(k):
    apart = lax.axis_index("col") ^ k
    return ((apart >> 1) & 3) | ((apart >> 1) & 4) | ((apart & 1) << 3)


def unpacked(ref, section):
    half = LANES // 2
    lower = lax.broadcasted_iota(jnp.int32, ref.shape[1:], 1) < half
    halves = []
    for k in range(ref.shape[0] // 2):
        even, odd = ref[block_at(2 * k)], ref[block_at(2 * k + 1)]
        if section == 0:
            odd = pltpu.roll(odd, half, 1)
        else:
            even = pltpu.roll(even, half, 1)
        halves.append(jnp.where(lower, even, odd))
    return jnp.concatenate(halves, 1)


def pair_kernel(gathered, src_ref, tgt_ref, out_ref, pair, force, tide, total):
    blocks, per = src_ref.shape[0], src_ref.shape[1] // 6 * LANES
    half = LANES // 2
    if gathered:
        info = unpacked(tgt_ref, 0)
        targets = rows(info[0:6], info[12:13], info[15:16])
    else:
        targets = tgt_ref[...]
    n_src, n_tgt = blocks * per, targets.shape[1]

    def prepare(i):
        for k in range(SRC_TILE // per):
            block = i * (SRC_TILE // per) + k
            cols = pl.ds(pl.multiple_of(block * per, per), per)
            packed = src_ref[block]
            state = jnp.concatenate([packed[6 * c : 6 * c + 6] for c in range(per // LANES)], 1)
            pair_rows, force[:, cols], tide[:, cols] = source_tables(state)
            pair[cols, :] = pair_rows.T

    lane = lax.broadcasted_iota(jnp.int32, (1, n_tgt), 1)
    slot = (lane & (half - 1)).astype(F32)
    offset = jnp.zeros((1, n_tgt), F32)
    live_count = jnp.zeros((1, 1), F32)
    for k in range(n_tgt // half):
        count = targets[6:7, k * half : k * half + 1]
        offset = offset + jnp.where(lane >= (k + 1) * half, count, 0.0)
        live_count = live_count + count
    place = jnp.where(slot < targets[6:7], offset + slot, -1.0).astype(jnp.int32)
    tiles = (jnp.max(live_count).astype(jnp.int32) + (TGT_TILE - 1)) // TGT_TILE
    total[...] = jnp.zeros_like(total)

    def target_tile(t, unused, make=None):
        spot = lax.broadcasted_iota(jnp.int32, (TGT_TILE, n_tgt), 0) + t * TGT_TILE
        pack = (spot == place).astype(F32).astype(BF16)
        sums = tile_sums((pair, force, tide), exact_dot(targets, pack, ((1,), (1,))), n_src, make)
        total[...] += exact_dot(sums, pack, ((1,), (0,)))
        return unused

    target_tile(0, 0, prepare)
    lax.fori_loop(1, tiles, target_tile, 0)
    if gathered:
        out_ref[0] = rows(*(total[0:6, k : k + LANES] for k in range(0, n_tgt, LANES)))
    else:
        for k in range(out_ref.shape[0]):
            out_ref[k] = total[:, k // 2 * LANES : (k // 2 + 1) * LANES]


def pair_sums(sources, targets, n_col):
    gathered = targets.ndim == 3
    n_src, n_tgt = sources.shape[0] * sources.shape[1] // 6 * LANES, n_col * LANES // 2
    pairs = n_src * n_tgt
    return pl.pallas_call(
        functools.partial(pair_kernel, gathered),
        out_shape=jax.ShapeDtypeStruct((1, 6 * n_tgt // LANES, LANES) if gathered else (n_col, 8, LANES), F32),
        in_specs=[pl.BlockSpec(memory_space=pltpu.VMEM)] * 2,
        out_specs=pl.BlockSpec(memory_space=pltpu.VMEM),
        scratch_shapes=[
            pltpu.VMEM((n_src, WIDE), BF16),
            pltpu.VMEM((32, n_src), BF16),
            pltpu.VMEM((16, n_src), BF16),
            pltpu.VMEM((8, n_tgt), F32),
        ],
        compiler_params=pltpu.CompilerParams(vmem_limit_bytes=VMEM_BYTES),
        cost_estimate=pl.CostEstimate(flops=600 * pairs, bytes_accessed=32 * (n_src + n_tgt), transcendentals=pairs),
        name="pair_sums",
    )(sources, targets)


def predict(pos, vel, acc, jerk, delta):
    new_pos = pos + delta * (vel + delta * (0.5 * acc + delta * jerk / 6.0))
    return new_pos, vel + delta * (acc + 0.5 * delta * jerk)


def correct(pos, vel, old_acc, old_jerk, acc, jerk, step):
    change = old_acc - acc
    snap = (-6.0 * change - step * (4.0 * old_jerk + 2.0 * jerk)) / (step * step)
    crackle = (12.0 * change + 6.0 * step * (old_jerk + jerk)) / (step * step * step)
    square = step * step
    fourth = square * square / 24.0
    new_pos = pos + fourth * snap + square * square * step / 120.0 * crackle
    return new_pos, vel + square * step / 6.0 * snap + fourth * crackle


def picked(low_slots, high_slots, stars):
    slots = jnp.concatenate([low_slots, high_slots], 1)
    return (lax.broadcasted_iota(jnp.int32, (stars, LANES), 0) == slots).astype(F32).astype(BF16)


def send_sources(pos, vel, src_ref):
    state = rows(pos, vel)
    packed = rows(*(state[:, k : k + LANES] for k in range(0, state.shape[1], LANES)))
    for k in range(src_ref.shape[0]):
        src_ref[k] = packed


def first_kernel(*refs):
    arrays, (src_ref, tgt_ref), held, sems = refs[:6], refs[6:8], refs[8:14], refs[14]
    copies = [pltpu.make_async_copy(a, b, sems.at[k]) for k, (a, b) in enumerate(zip(arrays, held))]
    for copy in copies:
        copy.start()
    for copy in copies:
        copy.wait()
    pos, vel, acc, jerk = (ref[...] for ref in held[:4])
    slots, count_ref = held[4][...], held[5]
    now = predict(pos, vel, acc, jerk, base_step)
    later = predict(pos, vel, acc, jerk, 2.0 * base_step)
    send_sources(*now, src_ref)
    lower = lax.broadcasted_iota(jnp.int32, (1, LANES), 1) < LANES // 2
    picks = picked(slots[0:1], slots[1:2], pos.shape[1])
    zero6 = jnp.zeros((6, pos.shape[1]), F32)
    own = exact_dot(rows(*now, *later, acc, jerk, zero6), picks, ((1,), (0,)))
    counts = jnp.where(lower, count_ref[0], count_ref[1]).astype(F32)
    slot = jnp.concatenate([slots[0:1], slots[1:2]], 1).astype(F32)
    target = rows(jnp.where(lower, own[0:6], own[6:12]), own[12:18], counts, slot, own[18:20])
    tgt_ref[0] = target


def middle_kernel(
    inv_mass, pos, vel, acc, jerk, slot_ref, parts_ref, info_ref,
    new_pos, new_vel, new_acc, new_jerk, src_ref, tgt_ref, own_ref,
):
    added = lambda first: sum(parts_ref[k] for k in range(first + 2, parts_ref.shape[0], 2)) + parts_ref[first]
    total = rows(added(0), added(1))
    forces = jnp.concatenate([total[k : k + 6] for k in range(0, total.shape[0], 6)], 1) * inv_mass
    active, after = unpacked(info_ref, 0), unpacked(info_ref, 1)
    n_tgt, half, stars = active.shape[1], LANES // 2, pos.shape[1]
    lane = lax.broadcasted_iota(jnp.int32, (1, n_tgt), 1)
    live = (lane & (half - 1)).astype(F32) < active[12:13]
    at_pos, at_vel = correct(active[0:3], active[3:6], active[6:9], active[9:12], forces[0:3], forces[3:6], base_step)
    one, zero3 = jnp.ones((1, n_tgt), F32), jnp.zeros((3, n_tgt), F32)
    fresh = jnp.where(live, rows(at_pos, at_vel, forces, one, zero3), 0.0)

    mine = jnp.where(lane // half == lax.axis_index("col"), active[13:14], -1.0).astype(jnp.int32)
    put = (lax.broadcasted_iota(jnp.int32, (stars, n_tgt), 0) == mine).astype(F32).astype(BF16)
    placed = exact_dot(fresh, put, ((1,), (1,)))
    moved = placed[12:13] > 0.5
    keep = lambda old, k: jnp.where(moved, placed[k : k + 3], old[...])
    state = (keep(pos, 0), keep(vel, 3), keep(acc, 6), keep(jerk, 9))
    for ref, value in zip((new_pos, new_vel, new_acc, new_jerk), state):
        ref[...] = value
    delta = jnp.where(moved, base_step, 2.0 * base_step)
    sources = predict(*state, delta)
    send_sources(*sources, src_ref)
    slots = slot_ref[1:2, :]
    zero = jnp.zeros((1, stars), F32)
    own = exact_dot(rows(*sources, *state[2:], delta, zero, zero, zero), picked(slots, slots, stars), ((1,), (0,)))
    count = jnp.broadcast_to(info_ref[0, 12:13, half : half + 1], (1, LANES))
    own_ref[...] = rows(own[0:13], count, own[13:15])

    moving = predict(fresh[0:3], fresh[3:6], fresh[6:9], fresh[9:12], base_step)
    moving = rows(*moving, fresh[12:14])
    was = jnp.where(live, active[13:14], -1.0) + (lane // half * stars).astype(F32)
    was = jnp.where(live, was, -1.0)
    will = after[13:14] + (lane // half * stars).astype(F32)
    span = 2 * LANES
    for k in range(0, n_tgt, span):
        cols = slice(k, k + span)
        column = jnp.broadcast_to(will[:, cols], (8, span)).T[:, 0:1]
        same = (column == was[:, cols]).astype(F32).astype(BF16)
        got = exact_dot(moving[:, cols], same, ((1,), (1,)))
        state = jnp.where(got[6:7] > 0.5, got[0:6], after[0:6, cols])
        tgt_ref[:, cols] = rows(state, after[12:13, cols], after[15:16, cols])


def last_kernel(
    inv_mass, pos, vel, acc, jerk, slot_ref, parts_ref, own_ref,
    new_pos, new_vel, new_acc, new_jerk,
):
    stars, half = pos.shape[1], LANES // 2
    total = parts_ref[0]
    for k in range(1, parts_ref.shape[0]):
        total = total + parts_ref[k]
    forces = total[0:6] * inv_mass
    own = own_ref[...]
    at_pos, at_vel = correct(own[0:3], own[3:6], own[6:9], own[9:12], forces[0:3], forces[3:6], own[12:13])
    lane = lax.broadcasted_iota(jnp.int32, (1, LANES), 1)
    first = (lax.axis_index("col") & 1) * half
    live = ((lane & (half - 1)).astype(F32) < own[13:14]) & (lane >= first) & (lane < first + half)
    fresh = rows(at_pos, at_vel, forces, jnp.ones((1, LANES), F32), jnp.zeros((3, LANES), F32))
    slots = slot_ref[1:2, :]
    placed = exact_dot(jnp.where(live, fresh, 0.0), picked(slots, slots, stars), ((1,), (1,)))
    moved = placed[12:13] > 0.5
    keep = lambda old, k: jnp.where(moved, placed[k : k + 3], old[...])
    new_pos[...], new_vel[...], new_acc[...], new_jerk[...] = keep(pos, 0), keep(vel, 3), keep(acc, 6), keep(jerk, 9)


def local_call(kernel, outs, operands, places, scratch=(), vmem=VMEM_BYTES, name=None):
    spec = lambda place: pl.BlockSpec(memory_space=place)
    return pl.pallas_call(
        kernel,
        out_shape=[jax.ShapeDtypeStruct(shape, F32) for shape in outs],
        in_specs=[spec(place) for place in places],
        out_specs=[spec(pltpu.VMEM)] * len(outs),
        scratch_shapes=list(scratch),
        compiler_params=pltpu.CompilerParams(vmem_limit_bytes=vmem),
        name=name,
    )(*operands)


def halved(sums, n_col):
    other = lax.ppermute(sums, "col", [(k, k ^ 1) for k in range(n_col)])
    size = sums.shape[1] // 2
    half = lax.dynamic_slice_in_dim(sums + other, (lax.axis_index("col") & 1) * size, size, 1)
    return lax.all_to_all(jnp.broadcast_to(half, (n_col, size, LANES)), "col", 0, 0)


def shards(positions, velocities, accel, jerks, act_slot, act_count):
    stars = positions.shape[1]
    n_row, n_col = lax.axis_size("row"), lax.axis_size("col")
    inv_mass = 1.0 / (stars * n_row * n_col)
    counts = act_count.reshape(-1)
    state = (positions, velocities, accel, jerks)
    like = [(3, stars)] * 4
    sources = (n_row, 6 * stars // LANES, LANES)

    everything = (*state, act_slot)
    held = [pltpu.VMEM(x.shape, x.dtype) for x in everything] + [pltpu.SMEM(counts.shape, counts.dtype), pltpu.SemaphoreType.DMA((6,))]
    src, tgt = local_call(
        first_kernel, [sources, (1, 16, LANES)], (*everything, counts), [pl.ANY] * 6, held, None, name="first"
    )
    src = lax.all_to_all(src, "row", 0, 0)
    info = tgt
    for masks in ROUNDS:
        others = [lax.ppermute(info, "col", [(k, k ^ mask) for k in range(n_col)]) for mask in masks]
        info = jnp.concatenate([info, *others])
    parts = halved(pair_sums(src, info, n_col), n_col)
    *state, src, tgt, own = local_call(
        functools.partial(middle_kernel, inv_mass), like + [sources, (8, n_col * LANES // 2), (16, LANES)],
        (*state, act_slot, parts, info), [pltpu.VMEM] * 7, name="middle",
    )
    src = lax.all_to_all(src, "row", 0, 0)
    parts = lax.all_to_all(pair_sums(src, tgt, n_col), "col", 0, 0)
    return tuple(
        local_call(
            functools.partial(last_kernel, inv_mass), like,
            (*state, act_slot, parts, own), [pltpu.VMEM] * 7, name="last",
        )
    )


def solution(mesh):
    placed = P(None, ("row", "col"))
    return jax.shard_map(shards, mesh=mesh, in_specs=(placed,) * 6, out_specs=(placed,) * 4, check_vma=False)
```

```python
import functools

import jax
import jax.numpy as jnp
from jax import lax
from jax.experimental import pallas as pl
from jax.experimental.pallas import tpu as pltpu
from jax.sharding import PartitionSpec as P

F32 = jnp.float32
BF16 = jnp.bfloat16

soften_sq = 0.01
base_step = 1.0 / 64.0
grid_step = 1.0 / 32.0

SRC_TILE = 4096
SRC_STEP = 256
TGT_TILE = 256
LANES = 128
WIDE = 80
VMEM_BYTES = 40 << 20
ROUNDS = ((2, 4, 6), (8,), (1,))


def rounded(x):
    return x.astype(BF16).astype(F32)


def split3(x):
    high = rounded(x)
    rest = x - high
    mid = rounded(rest)
    return high, mid, rounded(rest - mid)


def rows(*pieces):
    return jnp.concatenate(pieces, 0)


def exact_dot(values, picks, dims):
    count = values.shape[0]
    stacked = rows(*split3(values)).astype(BF16)
    got = lax.dot_general(stacked, picks, (dims, ((), ())), preferred_element_type=F32)
    return got[:count] + got[count : 2 * count] + got[2 * count :]


def pieces(state):
    grid = jnp.round(state * (1.0 / grid_step)) * grid_step
    fine = state - grid
    fine_high = rounded(fine)
    fine_low = rounded(fine - fine_high)
    pos, vel = slice(0, 3), slice(3, 6)
    add = lambda z: z[0:1] + z[1:2] + z[2:3]
    square = add(grid[pos] * grid[pos])
    square_rest = add((2.0 * grid[pos] + fine[pos]) * fine[pos])
    cross = add(grid[pos] * grid[vel])
    cross_rest = add(grid[pos] * fine[vel] + fine[pos] * grid[vel] + fine[pos] * fine[vel])
    return grid, fine_high, fine_low, square, square_rest, cross, cross_rest


def source_tables(state):
    grid, high, low, square, square_rest, cross, cross_rest = pieces(state)
    count = state.shape[1]
    one, zero = jnp.ones((1, count), F32), jnp.zeros((1, count), F32)
    zero6, zero8 = jnp.zeros((6, count), F32), jnp.zeros((8, count), F32)
    b_grid = rows(grid[0:6], one, zero)
    b_square = rows(*split3(square), *split3(cross), one, one)
    b_high = rows(high[0:6], one, one)
    b_low = rows(low[0:6], one, zero)
    b_rest = rows(*split3(square_rest), *split3(cross_rest), zero, zero)
    pair = rows(b_grid, b_square, b_high, b_low, b_grid, b_grid, b_high, b_low, b_high, b_rest)
    force = rows(b_grid, b_high, b_low, zero8)
    tide = rows(grid[0:3], high[0:3], low[0:3], one, zero6)
    return pair.astype(BF16), force.astype(BF16), tide.astype(BF16)


def target_tables(state):
    grid, high, low, square, square_rest, cross, cross_rest = pieces(state)
    count = state.shape[1]
    one, zero = jnp.ones((1, count), F32), jnp.zeros((1, count), F32)
    zero2, zero3 = jnp.zeros((2, count), F32), jnp.zeros((3, count), F32)

    def table(factor, units, main, rest):
        m, r = split3(main), split3(rest)
        fg, fh, fl = factor(grid), factor(high), factor(low)
        return rows(
            fg, m[0], zero, *units, m[1], m[2], fg, r[0], r[1], fg, r[2], zero,
            fh, zero2, fl, zero2, fh, zero2, fh, zero2, fl, zero2, *units, zero2,
        )

    distance = table(lambda c: rows(-2.0 * c[0:3], zero3), (one, one, one, zero3), square, square_rest + soften_sq)
    product = table(lambda c: rows(-c[3:6], -c[0:3]), (zero3, one, one, one), cross, cross_rest)
    return distance, product


def dot(a, b):
    return jnp.dot(a, b, preferred_element_type=F32)


def tile_at(i, k):
    first = i * SRC_TILE + k * SRC_STEP
    return pl.ds(first if isinstance(first, int) else pl.multiple_of(first, SRC_STEP), SRC_STEP)


def tile_sums(tables, targets, n_src, prepare=None):
    pair, force, tide = tables
    distance, product = target_tables(targets)
    distance, product = distance.astype(BF16), product.astype(BF16)

    def products(i, k):
        here = tile_at(i, k)
        left = pair[here, :]
        return dot(left, distance), dot(left, product)

    def collected(i, k, softened, radial, sums):
        here = tile_at(i, k)
        right, right_tide = force[:24, here], tide[:, here]
        root = lax.rsqrt(softened)
        inv_sq = root * root
        cube = inv_sq * root
        tidal = (radial * inv_sq) * cube
        cube_high, tidal_high = cube.astype(BF16), tidal.astype(BF16)
        cube_low = (cube - cube_high.astype(F32)).astype(BF16)
        tidal_low = (tidal - tidal_high.astype(F32)).astype(BF16)
        return (
            sums[0] + dot(right, cube_high) + dot(right, cube_low),
            sums[1] + dot(right_tide, tidal_high) + dot(right_tide, tidal_low),
        )

    def source_tile(i, sums, steps=SRC_TILE // SRC_STEP, before=None):
        ahead = products(i, 0)
        for k in range(steps):
            now = ahead
            if before is not None:
                before(k)
            if k + 1 < steps:
                ahead = products(i, k + 1)
            sums = collected(i, k, *now, sums)
        return sums

    zero = lambda count: jnp.zeros((count, targets.shape[1]), F32)
    start = (zero(24), zero(16))
    if prepare is None:
        forces, tides = lax.fori_loop(0, n_src // SRC_TILE, source_tile, start)
    else:
        per = 512 // SRC_STEP
        for block in range(4):
            prepare(block)
        before = lambda k: prepare(k // per + 4) if k % per == 0 and k // per + 4 < n_src // 512 else None
        forces, tides = source_tile(0, start, n_src // SRC_STEP, before)
    pulls = forces[0:8] + forces[8:16] + forces[16:24] - targets * forces[6:7]
    turns = (tides[0:3] + tides[3:6] + tides[6:9]) - targets[0:3] * tides[9:10]
    return rows(pulls[0:3], pulls[3:6] - 3.0 * turns, pulls[6:8])


def block_at(k):
    apart = lax.axis_index("col") ^ k
    return ((apart >> 1) & 3) | ((apart >> 1) & 4) | ((apart & 1) << 3)


def unpacked(ref, section):
    half = LANES // 2
    lower = lax.broadcasted_iota(jnp.int32, ref.shape[1:], 1) < half
    halves = []
    for k in range(ref.shape[0] // 2):
        even, odd = ref[block_at(2 * k)], ref[block_at(2 * k + 1)]
        if section == 0:
            odd = pltpu.roll(odd, half, 1)
        else:
            even = pltpu.roll(even, half, 1)
        halves.append(jnp.where(lower, even, odd))
    return jnp.concatenate(halves, 1)


def pair_kernel(gathered, src_ref, tgt_ref, out_ref, pair, force, tide, total):
    blocks, per = src_ref.shape[0], src_ref.shape[1] // 6 * LANES
    half = LANES // 2
    if gathered:
        info = unpacked(tgt_ref, 0)
        targets = rows(info[0:6], info[12:13], info[15:16])
    else:
        targets = tgt_ref[...]
    n_src, n_tgt = blocks * per, targets.shape[1]

    def prepare(block):
        cols = slice(block * per, block * per + per)
        packed = src_ref[block]
        state = jnp.concatenate([packed[6 * c : 6 * c + 6] for c in range(per // LANES)], 1)
        pair_rows, force[:, cols], tide[:, cols] = source_tables(state)
        pair[cols, :] = pair_rows.T

    lane = lax.broadcasted_iota(jnp.int32, (1, n_tgt), 1)
    slot = (lane & (half - 1)).astype(F32)
    offset = jnp.zeros((1, n_tgt), F32)
    live_count = jnp.zeros((1, 1), F32)
    for k in range(n_tgt // half):
        count = targets[6:7, k * half : k * half + 1]
        offset = offset + jnp.where(lane >= (k + 1) * half, count, 0.0)
        live_count = live_count + count
    place = jnp.where(slot < targets[6:7], offset + slot, -1.0).astype(jnp.int32)
    tiles = (jnp.max(live_count).astype(jnp.int32) + (TGT_TILE - 1)) // TGT_TILE
    total[...] = jnp.zeros_like(total)

    def target_tile(t, unused, make=None):
        spot = lax.broadcasted_iota(jnp.int32, (TGT_TILE, n_tgt), 0) + t * TGT_TILE
        pack = (spot == place).astype(F32).astype(BF16)
        sums = tile_sums((pair, force, tide), exact_dot(targets, pack, ((1,), (1,))), n_src, make)
        total[...] += exact_dot(sums, pack, ((1,), (0,)))
        return unused

    target_tile(0, 0, prepare)
    lax.fori_loop(1, tiles, target_tile, 0)
    if gathered:
        out_ref[0] = rows(*(total[0:6, k : k + LANES] for k in range(0, n_tgt, LANES)))
    else:
        for k in range(out_ref.shape[0]):
            out_ref[k] = total[:, k // 2 * LANES : (k // 2 + 1) * LANES]


def pair_sums(sources, targets, n_col):
    gathered = targets.ndim == 3
    n_src, n_tgt = sources.shape[0] * sources.shape[1] // 6 * LANES, n_col * LANES // 2
    pairs = n_src * n_tgt
    return pl.pallas_call(
        functools.partial(pair_kernel, gathered),
        out_shape=jax.ShapeDtypeStruct((1, 6 * n_tgt // LANES, LANES) if gathered else (n_col, 8, LANES), F32),
        in_specs=[pl.BlockSpec(memory_space=pltpu.VMEM)] * 2,
        out_specs=pl.BlockSpec(memory_space=pltpu.VMEM),
        scratch_shapes=[
            pltpu.VMEM((n_src, WIDE), BF16),
            pltpu.VMEM((32, n_src), BF16),
            pltpu.VMEM((16, n_src), BF16),
            pltpu.VMEM((8, n_tgt), F32),
        ],
        compiler_params=pltpu.CompilerParams(vmem_limit_bytes=VMEM_BYTES),
        cost_estimate=pl.CostEstimate(flops=600 * pairs, bytes_accessed=32 * (n_src + n_tgt), transcendentals=pairs),
        name="pair_sums",
    )(sources, targets)


def predict(pos, vel, acc, jerk, delta):
    new_pos = pos + delta * (vel + delta * (0.5 * acc + delta * jerk / 6.0))
    return new_pos, vel + delta * (acc + 0.5 * delta * jerk)


def correct(pos, vel, old_acc, old_jerk, acc, jerk, step):
    change = old_acc - acc
    snap = (-6.0 * change - step * (4.0 * old_jerk + 2.0 * jerk)) / (step * step)
    crackle = (12.0 * change + 6.0 * step * (old_jerk + jerk)) / (step * step * step)
    square = step * step
    fourth = square * square / 24.0
    new_pos = pos + fourth * snap + square * square * step / 120.0 * crackle
    return new_pos, vel + square * step / 6.0 * snap + fourth * crackle


def picked(low_slots, high_slots, stars):
    slots = jnp.concatenate([low_slots, high_slots], 1)
    return (lax.broadcasted_iota(jnp.int32, (stars, LANES), 0) == slots).astype(F32).astype(BF16)


def send_sources(pos, vel, src_ref):
    state = rows(pos, vel)
    packed = rows(*(state[:, k : k + LANES] for k in range(0, state.shape[1], LANES)))
    for k in range(src_ref.shape[0]):
        src_ref[k] = packed


def first_kernel(*refs):
    arrays, (src_ref, tgt_ref), held, sems = refs[:6], refs[6:8], refs[8:14], refs[14]
    copies = [pltpu.make_async_copy(a, b, sems.at[k]) for k, (a, b) in enumerate(zip(arrays, held))]
    for copy in copies:
        copy.start()
    for copy in copies:
        copy.wait()
    pos, vel, acc, jerk = (ref[...] for ref in held[:4])
    slots, count_ref = held[4][...], held[5]
    now = predict(pos, vel, acc, jerk, base_step)
    later = predict(pos, vel, acc, jerk, 2.0 * base_step)
    send_sources(*now, src_ref)
    lower = lax.broadcasted_iota(jnp.int32, (1, LANES), 1) < LANES // 2
    picks = picked(slots[0:1], slots[1:2], pos.shape[1])
    zero6 = jnp.zeros((6, pos.shape[1]), F32)
    own = exact_dot(rows(*now, *later, acc, jerk, zero6), picks, ((1,), (0,)))
    counts = jnp.where(lower, count_ref[0], count_ref[1]).astype(F32)
    slot = jnp.concatenate([slots[0:1], slots[1:2]], 1).astype(F32)
    target = rows(jnp.where(lower, own[0:6], own[6:12]), own[12:18], counts, slot, own[18:20])
    tgt_ref[0] = target


def middle_kernel(
    inv_mass, pos, vel, acc, jerk, slot_ref, parts_ref, info_ref,
    new_pos, new_vel, new_acc, new_jerk, src_ref, tgt_ref, own_ref,
):
    added = lambda first: sum(parts_ref[k] for k in range(first + 2, parts_ref.shape[0], 2)) + parts_ref[first]
    total = rows(added(0), added(1))
    forces = jnp.concatenate([total[k : k + 6] for k in range(0, total.shape[0], 6)], 1) * inv_mass
    active, after = unpacked(info_ref, 0), unpacked(info_ref, 1)
    n_tgt, half, stars = active.shape[1], LANES // 2, pos.shape[1]
    lane = lax.broadcasted_iota(jnp.int32, (1, n_tgt), 1)
    live = (lane & (half - 1)).astype(F32) < active[12:13]
    at_pos, at_vel = correct(active[0:3], active[3:6], active[6:9], active[9:12], forces[0:3], forces[3:6], base_step)
    one, zero3 = jnp.ones((1, n_tgt), F32), jnp.zeros((3, n_tgt), F32)
    fresh = jnp.where(live, rows(at_pos, at_vel, forces, one, zero3), 0.0)

    mine = jnp.where(lane // half == lax.axis_index("col"), active[13:14], -1.0).astype(jnp.int32)
    put = (lax.broadcasted_iota(jnp.int32, (stars, n_tgt), 0) == mine).astype(F32).astype(BF16)
    placed = exact_dot(fresh, put, ((1,), (1,)))
    moved = placed[12:13] > 0.5
    keep = lambda old, k: jnp.where(moved, placed[k : k + 3], old[...])
    state = (keep(pos, 0), keep(vel, 3), keep(acc, 6), keep(jerk, 9))
    for ref, value in zip((new_pos, new_vel, new_acc, new_jerk), state):
        ref[...] = value
    delta = jnp.where(moved, base_step, 2.0 * base_step)
    sources = predict(*state, delta)
    send_sources(*sources, src_ref)
    slots = slot_ref[1:2, :]
    zero = jnp.zeros((1, stars), F32)
    own = exact_dot(rows(*sources, *state[2:], delta, zero, zero, zero), picked(slots, slots, stars), ((1,), (0,)))
    count = jnp.broadcast_to(info_ref[0, 12:13, half : half + 1], (1, LANES))
    own_ref[...] = rows(own[0:13], count, own[13:15])

    moving = predict(fresh[0:3], fresh[3:6], fresh[6:9], fresh[9:12], base_step)
    moving = rows(*moving, fresh[12:14])
    was = jnp.where(live, active[13:14], -1.0) + (lane // half * stars).astype(F32)
    was = jnp.where(live, was, -1.0)
    will = after[13:14] + (lane // half * stars).astype(F32)
    span = 2 * LANES
    for k in range(0, n_tgt, span):
        cols = slice(k, k + span)
        column = jnp.broadcast_to(will[:, cols], (8, span)).T[:, 0:1]
        same = (column == was[:, cols]).astype(F32).astype(BF16)
        got = exact_dot(moving[:, cols], same, ((1,), (1,)))
        state = jnp.where(got[6:7] > 0.5, got[0:6], after[0:6, cols])
        tgt_ref[:, cols] = rows(state, after[12:13, cols], after[15:16, cols])


def last_kernel(
    inv_mass, pos, vel, acc, jerk, slot_ref, parts_ref, own_ref,
    new_pos, new_vel, new_acc, new_jerk,
):
    stars, half = pos.shape[1], LANES // 2
    total = parts_ref[0]
    for k in range(1, parts_ref.shape[0]):
        total = total + parts_ref[k]
    forces = total[0:6] * inv_mass
    own = own_ref[...]
    at_pos, at_vel = correct(own[0:3], own[3:6], own[6:9], own[9:12], forces[0:3], forces[3:6], own[12:13])
    lane = lax.broadcasted_iota(jnp.int32, (1, LANES), 1)
    first = (lax.axis_index("col") & 1) * half
    live = ((lane & (half - 1)).astype(F32) < own[13:14]) & (lane >= first) & (lane < first + half)
    fresh = rows(at_pos, at_vel, forces, jnp.ones((1, LANES), F32), jnp.zeros((3, LANES), F32))
    slots = slot_ref[1:2, :]
    placed = exact_dot(jnp.where(live, fresh, 0.0), picked(slots, slots, stars), ((1,), (1,)))
    moved = placed[12:13] > 0.5
    keep = lambda old, k: jnp.where(moved, placed[k : k + 3], old[...])
    new_pos[...], new_vel[...], new_acc[...], new_jerk[...] = keep(pos, 0), keep(vel, 3), keep(acc, 6), keep(jerk, 9)


def local_call(kernel, outs, operands, places, scratch=(), vmem=VMEM_BYTES, name=None):
    spec = lambda place: pl.BlockSpec(memory_space=place)
    return pl.pallas_call(
        kernel,
        out_shape=[jax.ShapeDtypeStruct(shape, F32) for shape in outs],
        in_specs=[spec(place) for place in places],
        out_specs=[spec(pltpu.VMEM)] * len(outs),
        scratch_shapes=list(scratch),
        compiler_params=pltpu.CompilerParams(vmem_limit_bytes=vmem),
        name=name,
    )(*operands)


def halved(sums, n_col):
    other = lax.ppermute(sums, "col", [(k, k ^ 1) for k in range(n_col)])
    size = sums.shape[1] // 2
    half = lax.dynamic_slice_in_dim(sums + other, (lax.axis_index("col") & 1) * size, size, 1)
    return lax.all_to_all(jnp.broadcast_to(half, (n_col, size, LANES)), "col", 0, 0)


def shards(positions, velocities, accel, jerks, act_slot, act_count):
    stars = positions.shape[1]
    n_row, n_col = lax.axis_size("row"), lax.axis_size("col")
    inv_mass = 1.0 / (stars * n_row * n_col)
    counts = act_count.reshape(-1)
    state = (positions, velocities, accel, jerks)
    like = [(3, stars)] * 4
    sources = (n_row, 6 * stars // LANES, LANES)

    everything = (*state, act_slot)
    held = [pltpu.VMEM(x.shape, x.dtype) for x in everything] + [pltpu.SMEM(counts.shape, counts.dtype), pltpu.SemaphoreType.DMA((6,))]
    src, tgt = local_call(
        first_kernel, [sources, (1, 16, LANES)], (*everything, counts), [pl.ANY] * 6, held, None, name="first"
    )
    src = lax.all_to_all(src, "row", 0, 0)
    info = tgt
    for masks in ROUNDS:
        others = [lax.ppermute(info, "col", [(k, k ^ mask) for k in range(n_col)]) for mask in masks]
        info = jnp.concatenate([info, *others])
    parts = halved(pair_sums(src, info, n_col), n_col)
    *state, src, tgt, own = local_call(
        functools.partial(middle_kernel, inv_mass), like + [sources, (8, n_col * LANES // 2), (16, LANES)],
        (*state, act_slot, parts, info), [pltpu.VMEM] * 7, name="middle",
    )
    src = lax.all_to_all(src, "row", 0, 0)
    parts = lax.all_to_all(pair_sums(src, tgt, n_col), "col", 0, 0)
    return tuple(
        local_call(
            functools.partial(last_kernel, inv_mass), like,
            (*state, act_slot, parts, own), [pltpu.VMEM] * 7, name="last",
        )
    )


def solution(mesh):
    placed = P(None, ("row", "col"))
    return jax.shard_map(shards, mesh=mesh, in_specs=(placed,) * 6, out_specs=(placed,) * 4, check_vma=False)
```
